128 devices in a mesh: cls: 4 (over x_hi, core), img: 32 (over x_lo, z, y).
Axes of the slice: x: 4 (x_hi: 2, x_lo: 2; x = x_hi * 2 + x_lo), y: 4, z: 4, core: 2. Of those that a mesh axis runs over, the one named last changes fastest.
Arguments:
- particles: float32 [4096, 4096], P(('cls', 'img')), may hold values from -48 to 48
- rot_prior: int32 [4096], P(('cls', 'img')), may hold values from 0 to 11
- panels: bfloat16 [100, 12, 4096], P('cls', None, 'img'), may hold values from -4.5 to 4.5
- log_prior: float32 [100], P('cls'), may hold values from -0.5 to 3.7
- shift_table: int32 [11, 2], replicated, may hold values from -4 to 4, as said below
Outputs:
- class_sums: float32 [100, 12, 4096], P('cls', None, 'img')
- weight_totals: float32 [100, 12], P('cls')
- log_evidence: float32 [4096], P(('cls', 'img'))
The draws below stay inside these ranges and needn't reach their ends.
Inputs may be any that keep to these rules, and one draw needn't show every extreme that they name: `shift_table`: the 11 rows are distinct offsets; each entry lies within -4 to 4.
All inputs are finite; a program needn't handle non-finite values.
Results may differ from the reference program's by a relative error of at most 0.0085.
Values may be sent and summed in bfloat16 or wider, within the bound.
No kernel may reach another device: no remote copies, remote signals or barrier semaphores. Data moves between devices by JAX's collectives and lax.ppermute only.
A program may use at most 128 MiB of HBM per device.

```python
import math
import jax
import jax.numpy as jnp
from jax import lax

SIDE = 64
PIX = 4096
ROT = 12
SHIFTS = 11
CLASSES = 100
PARTICLES = 4096


def panel_base(key):
    grid = jax.random.normal(key, (CLASSES * ROT, PIX), jnp.float32)
    return grid


def draw_panels(key, part):
    grid = panel_base(key)
    values = jnp.clip(grid, -4.5, 4.5)
    return values.reshape(CLASSES, ROT, PIX).astype(jnp.bfloat16)


def draw_particles(key, part):
    grid = panel_base(key)
    key = jax.random.fold_in(key, 13)
    first_key = jax.random.fold_in(key, 0)
    third_key = jax.random.fold_in(key, 2)
    first_panel = jax.random.randint(third_key, (PARTICLES,), 0, CLASSES * ROT)
    row_index = jnp.arange(PARTICLES, dtype=jnp.int32)
    target = 150.0 + 50.0 * (row_index % 4).astype(jnp.float32)
    level = target / (2.5 * math.sqrt(PIX))
    chosen = (row_index % 37 == 5)[:, None]
    background = jnp.clip(jax.random.normal(first_key, (PARTICLES, PIX), jnp.float32), -4.5, 4.5)
    aligned = (0.5 + level)[:, None] * jnp.clip(grid[first_panel], -4.5, 4.5)
    return jnp.where(chosen, aligned, background)


def draw_log_prior(key, part):
    key = jax.random.fold_in(key, 14)
    ramp = jnp.arange(CLASSES, dtype=jnp.float32) / CLASSES
    jitter = jax.random.uniform(key, (CLASSES,), jnp.float32, -0.5, 0.5)
    return 1.6 * ramp + jitter


def draw_shift_table(key, part):
    key = jax.random.fold_in(key, 15)
    pick_key, order_key = jax.random.split(key)
    others = jnp.arange(78, dtype=jnp.int32) + 1
    others = others + (others >= 40).astype(jnp.int32)
    chosen = jax.random.permutation(pick_key, others)[:SHIFTS - 3]
    fixed_ids = jnp.array([0, 40, 80], dtype=jnp.int32)
    offset_ids = jax.random.permutation(order_key, jnp.concatenate([fixed_ids, chosen]))
    return jnp.stack([offset_ids // 9 - 4, offset_ids % 9 - 4], axis=1).astype(jnp.int32)


def with_ends(values, rng, smallest, largest):
    longest = values.shape.index(max(values.shape))
    spots = []
    for shift in (0, 1):
        where = [jax.random.randint(jax.random.fold_in(rng, axis), (), 0, length) for axis, length in enumerate(values.shape)]
        where[longest] = (where[longest] + shift) % values.shape[longest]
        spots.append(tuple(where))
    return values.at[spots[0]].set(smallest).at[spots[1]].set(largest)


def setup_inputs(seed: int = 0) -> dict:
    arg_keys = jax.random.split(jax.random.key(seed), 6)
    return {
        "particles": draw_particles(jax.random.fold_in(arg_keys[5], 71), 0),
        "rot_prior": with_ends(jax.random.randint(arg_keys[1], (PARTICLES,), 0, ROT), jax.random.fold_in(arg_keys[1], 1), 0, ROT - 1).astype(jnp.int32),
        "panels": draw_panels(jax.random.fold_in(arg_keys[5], 71), 0),
        "log_prior": draw_log_prior(jax.random.fold_in(arg_keys[5], 71), 0),
        "shift_table": draw_shift_table(jax.random.fold_in(arg_keys[5], 71), 0),
    }


SCORE_GAIN = 2.5
PRIOR_WEIGHT = 1.0

def shifted_images(images, offset, image_side):
    count = images.shape[0]
    square = images.reshape(count, image_side, image_side)
    moved = jnp.roll(square, (-offset[0], -offset[1]), axis=(1, 2))
    return moved.reshape(count, image_side * image_side)

def score_block(images, rotations, flat_panels, panel_bias, shift_table, image_side, rot_count, score_gain):
    columns = []
    for offset_index in range(shift_table.shape[0]):
        moved = shifted_images(images, shift_table[offset_index], image_side)
        columns.append(lax.dot_general(moved, flat_panels, (((1,), (1,)), ((), ())), preferred_element_type=jnp.float32))
    stacked = jnp.stack(columns, axis=1)
    panel_rotation = jnp.arange(flat_panels.shape[0], dtype=jnp.int32) % rot_count
    angle = 2.0 * math.pi / rot_count * (panel_rotation[None, :] - rotations[:, None]).astype(jnp.float32)
    prior_term = PRIOR_WEIGHT * jnp.cos(angle)
    return score_gain * stacked + panel_bias[None, None, :] + prior_term[:, None, :]

def reference(particles, rot_prior, panels, log_prior, shift_table):
    panel_count = CLASSES * ROT
    flat_panels = panels.reshape(panel_count, PIX)
    score_gain = SCORE_GAIN / math.sqrt(PIX)
    norms = lax.optimization_barrier(jnp.sum(jnp.square(flat_panels.astype(jnp.float32)), axis=1))
    panel_bias = jnp.repeat(log_prior, ROT) - 0.5 * score_gain * norms
    block_rows = math.gcd(PARTICLES, 512)
    block_count = PARTICLES // block_rows
    image_blocks = particles.astype(jnp.bfloat16).reshape(block_count, block_rows, PIX)
    rot_blocks = rot_prior.reshape(block_count, block_rows)

    def one_block(carry, inputs):
        sums_now, totals_now = carry
        images, rotations = inputs
        scores = score_block(images, rotations, flat_panels, panel_bias, shift_table, SIDE, ROT, score_gain)
        peak = lax.optimization_barrier(jnp.max(scores, axis=(1, 2)))
        total = lax.optimization_barrier(jnp.sum(jnp.exp(scores - peak[:, None, None]), axis=(1, 2)))
        evidence = peak + jnp.log(total)
        weights = (jnp.exp(scores - peak[:, None, None]) / total[:, None, None]).astype(jnp.bfloat16)
        totals_now = totals_now + lax.optimization_barrier(jnp.sum(weights.astype(jnp.float32), axis=(0, 1)))
        for offset_index in range(SHIFTS):
            moved = shifted_images(images, shift_table[offset_index], SIDE)
            sums_now = sums_now + lax.dot_general(weights[:, offset_index, :], moved, (((0,), (0,)), ((), ())), preferred_element_type=jnp.float32)
        return ((sums_now, totals_now), evidence)
    start = (jnp.zeros((panel_count, PIX), jnp.float32), jnp.zeros((panel_count,), jnp.float32))
    (sums_all, totals_all), evidence_blocks = lax.scan(one_block, start, (image_blocks, rot_blocks))
    return (sums_all.reshape(CLASSES, ROT, PIX), totals_all.reshape(CLASSES, ROT), evidence_blocks.reshape(PARTICLES))
```

```python
import math

import jax
import jax.numpy as jnp
from jax import lax
from jax.experimental import pallas as pl
from jax.experimental.pallas import tpu as pltpu
from jax.sharding import PartitionSpec as P

SCORE_GAIN = 2.5
PRIOR_WEIGHT = 1.0
AXES = ("cls", "img")
SIDE = 64
PIX = SIDE * SIDE
LANES = 128
BLOCKS = PIX // LANES
ROT = 12
HALF_ROT = ROT // 2
CLS = 25
USED = HALF_ROT * CLS
ROWS = 160
OWN = 32
ROW_IMAGES = 8 * OWN
SHIFTS = 11
MARGIN = 8
NEG = -1.0e30
Z_ORDER = (0, -1, 1, 2)


def flat(x, core, z, y):
    x %= 4
    return ((x // 2) * 2 + core % 2) * 32 + (x % 2) * 16 + (z % 4) * 4 + y % 4


COORDS = [(x, c, z, y) for x in range(4) for c in range(2) for z in range(4) for y in range(4)]
X_ROWS = [[flat(x, c, z, y) for x in range(4) for c in range(2)] for z in range(4) for y in range(4)]


def move(value, x=0, core=0, z=0, y=0):
    route = [(flat(*a), flat(a[0] + x, a[1] + core, a[2] + z, a[3] + y)) for a in COORDS]
    return lax.ppermute(value, AXES, route)


def swap_x(value):
    route = [(flat(x, c, z, y), flat(x ^ 1, c, z, y)) for x, c, z, y in COORDS]
    return lax.ppermute(value, AXES, route)


def position():
    cls, img = lax.axis_index("cls"), lax.axis_index("img")
    x_lo, z, y = img // 16, (img // 4) % 4, img % 4
    return (cls // 2) * 2 + x_lo, cls % 2, x_lo, z, y


def shifted_pixels(t_ref, rows, dy, dx):
    parts = []
    for row in rows:
        at = jnp.bitwise_and(row + dy, SIDE - 1)
        tiles = [t_ref[t, at, pl.ds(MARGIN + dx, SIDE), :] for t in range(2)]
        parts.append(jnp.concatenate(tiles, axis=1).astype(jnp.bfloat16))
    return jnp.concatenate(parts, axis=0)


def score_kernel(shift_ref, *refs):
    images = refs[:10]
    pc, py1, py3, pw0, pw1, info_ref, e_ref, st_ref, t_ref, x_ref = refs[10:]
    x, core, x_lo, z, y = position()
    gain = SCORE_GAIN / math.sqrt(PIX)

    def put(ref, dx, dc, part=0):
        slot = jnp.bitwise_and(x + dx, 3) * 2 + jnp.bitwise_xor(core, dc)
        start = pl.multiple_of(slot * OWN + part * 16, 16)
        x_ref[pl.ds(start, ref.shape[0]), :] = ref[...]

    own, a1, a2, c0, b1, b2, c1, c2, d1, d2 = images
    put(own, 0, 0)
    put(a1, -1, 0)
    put(a2, 1, 0)
    put(c0, 0, 1)
    put(c1, -1, 1)
    put(c2, 1, 1)
    put(b1, 2, 0, 0)
    put(b2, 2, 0, 1)
    put(d1, 2, 1, 0)
    put(d2, 2, 1, 1)

    def transpose_block(block, carry):
        for t in range(2):
            lanes = pl.ds(pl.multiple_of(block * LANES, LANES), LANES)
            tile = x_ref[pl.ds(t * LANES, LANES), lanes].astype(jnp.float32).T
            for half in range(2):
                line = tile[half * SIDE : (half + 1) * SIDE]
                t_ref[t, 2 * block + half, pl.ds(MARGIN, SIDE), :] = line
                t_ref[t, 2 * block + half, pl.ds(0, MARGIN), :] = line[SIDE - MARGIN :]
                t_ref[t, 2 * block + half, pl.ds(MARGIN + SIDE, MARGIN), :] = line[:MARGIN]
        return carry

    lax.fori_loop(0, BLOCKS, transpose_block, 0)

    pairs = [(pc, 2 * i, dz, 0) for i, dz in enumerate(Z_ORDER)]
    pairs += [(py1, 2 * i, dz, -1) for i, dz in enumerate(Z_ORDER)]
    pairs += [(py3, 2 * i, dz, 1) for i, dz in enumerate(Z_ORDER)]
    pairs += [(pw0, 2 * i, dz, 2) for i, dz in enumerate(Z_ORDER[:2])]
    pairs += [(pw1, 2 * i, dz, 2) for i, dz in enumerate(Z_ORDER[2:])]

    squares = jnp.zeros((ROWS, LANES), jnp.float32)
    for ref, at, _, _ in pairs:
        for k in range(2):
            value = ref[at + k].astype(jnp.float32)
            squares = squares + value * value
    norms = jnp.sum(squares, axis=1, keepdims=True)
    rots = [
        x_ref[pl.ds(t * LANES, LANES), PIX : PIX + LANES].astype(jnp.float32).T[0:1]
        for t in range(2)
    ]
    angle = jnp.concatenate(rots, axis=1) * (2.0 * math.pi / ROT)
    info = info_ref[...]
    prior = info[:, 1:2] * jnp.cos(angle) + info[:, 2:3] * jnp.sin(angle)
    bias = info[:, 0:1] - 0.5 * gain * norms + PRIOR_WEIGHT * prior

    def one_shift(s, peak):
        dy, dx = shift_ref[s, 0], shift_ref[s, 1]
        acc = jnp.zeros((ROWS, ROW_IMAGES), jnp.float32)
        for ref, at, dz, dyy in pairs:
            base = jnp.bitwise_and(z + dz, 3) * 4 + jnp.bitwise_and(y + dyy, 3)
            j0 = x_lo * 16 + base
            j1 = (1 - x_lo) * 16 + base
            moved = shifted_pixels(t_ref, (2 * j0, 2 * j0 + 1, 2 * j1, 2 * j1 + 1), dy, dx)
            panel = jnp.concatenate([ref[at], ref[at + 1]], axis=1)
            acc = acc + jnp.dot(panel, moved, preferred_element_type=jnp.float32)
        scores = gain * acc + bias
        e_ref[s] = scores
        return jnp.maximum(peak, jnp.max(scores, axis=0, keepdims=True))

    peak = lax.fori_loop(0, SHIFTS, one_shift, jnp.full((1, ROW_IMAGES), NEG, jnp.float32))

    def one_exp(s, total):
        value = jnp.exp(e_ref[s] - peak)
        e_ref[s] = value
        return total + jnp.sum(value, axis=0, keepdims=True)

    total = lax.fori_loop(0, SHIFTS, one_exp, jnp.zeros((1, ROW_IMAGES), jnp.float32))
    stats = jnp.concatenate(
        [
            peak[:, :LANES],
            peak[:, LANES:],
            total[:, :LANES],
            total[:, LANES:],
            jnp.zeros((4, LANES), jnp.float32),
        ],
        axis=0,
    )
    for k in range(8):
        st_ref[k] = stats


def sum_kernel(shift_ref, e_ref, st_ref, all_ref, t_ref, out_ref, ev_ref, w_ref):
    x, core, _, _, _ = position()
    stats = [all_ref[k] for k in range(8)]
    peak = stats[0][0:2]
    for k in range(1, 8):
        peak = jnp.maximum(peak, stats[k][0:2])
    total = jnp.zeros((2, LANES), jnp.float32)
    for k in range(8):
        total = total + stats[k][2:4] * jnp.exp(stats[k][0:2] - peak)
    evidence = peak + jnp.log(total)
    slot = x * 2 + core
    mine = jnp.where(slot >= 4, evidence[1:2], evidence[0:1])
    groups = [mine[:, k * OWN : (k + 1) * OWN] for k in range(4)]
    at = jnp.bitwise_and(slot, 3)
    picked = groups[0]
    for k in range(1, 4):
        picked = jnp.where(at == k, groups[k], picked)
    ev_ref[...] = picked
    factor = jnp.exp(st_ref[0][0:2] - peak) / total
    factor = jnp.concatenate([factor[0:1], factor[1:2]], axis=1)

    def one_weight(s, totals):
        weight = (e_ref[s] * factor).astype(jnp.bfloat16)
        w_ref[s] = weight
        ones = jnp.ones((8, ROW_IMAGES), jnp.bfloat16)
        return totals + lax.dot_general(
            ones, weight, (((1,), (1,)), ((), ())), preferred_element_type=jnp.float32
        )

    totals = lax.fori_loop(0, SHIFTS, one_weight, jnp.zeros((8, ROWS), jnp.float32))[0:1]
    totals = jnp.concatenate([totals, jnp.zeros((1, 2 * LANES - ROWS), jnp.float32)], axis=1)
    pieces = []
    for _ in range(3):
        part = totals.astype(jnp.bfloat16).astype(jnp.float32)
        totals = totals - part
        pieces += [part[:, :LANES], part[:, LANES:]]
    tail = jnp.concatenate(
        [jnp.zeros((6, LANES), jnp.float32)] + pieces + [jnp.zeros((4, LANES), jnp.float32)], axis=0
    )

    def one_block(pair, carry):
        rows = tuple(4 * pair + k for k in range(4))
        acc = jnp.zeros((ROWS, 2 * LANES), jnp.float32)
        for s in range(SHIFTS):
            moved = shifted_pixels(t_ref, rows, shift_ref[s, 0], shift_ref[s, 1])
            acc = acc + lax.dot_general(
                w_ref[s], moved, (((1,), (1,)), ((), ())), preferred_element_type=jnp.float32
            )
        for k in range(2):
            part = acc[:, k * LANES : (k + 1) * LANES]
            out_ref[2 * pair + k, 0 : ROWS - 16, :] = part[: ROWS - 16].astype(jnp.bfloat16)
            out_ref[2 * pair + k, ROWS - 16 : ROWS, :] = (part[ROWS - 16 :] + tail).astype(
                jnp.bfloat16
            )
        return carry

    lax.fori_loop(0, BLOCKS // 2, one_block, 0)


def finish_kernel(in_ref, out_ref, wt_ref):
    for half in range(2):
        acc = jnp.zeros((ROWS, LANES), jnp.float32)
        for k in range(16):
            acc = acc + in_ref[half * 16 + k].astype(jnp.float32)
        for r in range(HALF_ROT):
            out_ref[half * HALF_ROT + r] = acc[r * CLS : (r + 1) * CLS]
        wide = [
            acc[USED + k : USED + k + 1] + acc[USED + 2 + k : USED + 3 + k]
            + acc[USED + 4 + k : USED + 5 + k]
            for k in range(2)
        ]
        totals = jnp.concatenate(wide, axis=1)
        for r in range(HALF_ROT):
            row = half * HALF_ROT + r
            wt_ref[row : row + 1, :] = totals[:, r * CLS : (r + 1) * CLS]


VMEM = pl.BlockSpec(memory_space=pltpu.VMEM)
SMEM = pl.BlockSpec(memory_space=pltpu.SMEM)
PARAMS = pltpu.CompilerParams(vmem_limit_bytes=40 * 1024 * 1024)


def shards(particles, rot_prior, panels, log_prior, shift_table):
    x_lo = lax.axis_index("img") // 16

    by_rot = jnp.transpose(panels, (1, 0, 2)).reshape(2, USED, LANES)
    by_rot = jnp.pad(by_rot, ((0, 0), (0, ROWS - USED), (0, 0)))
    keep = jnp.where(x_lo == 0, by_rot[0], by_rot[1])
    give = jnp.where(x_lo == 0, by_rot[1], by_rot[0])
    images = jnp.concatenate(
        [
            particles.astype(jnp.bfloat16),
            jnp.broadcast_to(rot_prior.astype(jnp.bfloat16)[:, None], (OWN, LANES)),
        ],
        axis=1,
    )
    got = swap_x(give)
    a1 = move(images, x=1)
    a2 = move(images, x=-1)
    c0 = move(images, core=1)
    first = jnp.stack([keep, got])
    u = move(first, z=1)
    v = move(first, z=-1)
    b1 = move(a1[:16], x=1)
    b2 = move(a2[16:], x=-1)
    w0 = move(u[0], z=1)
    w1 = move(v[1], z=-1)
    c1 = move(a1, core=1)
    c2 = move(a2, core=1)
    column = jnp.concatenate([first, u, v, w0[None], w1[None]], axis=0)
    y1 = move(column, y=1)
    y3 = move(column, y=-1)
    d1 = move(b1, core=1)
    d2 = move(b2, core=1)
    yw0 = move(y1[:4], y=1)
    yw1 = move(y3[4:], y=-1)

    row = jnp.arange(ROWS)
    rot = (row // CLS + HALF_ROT * x_lo).astype(jnp.float32) * (2.0 * math.pi / ROT)
    logs = jnp.pad(jnp.tile(log_prior, HALF_ROT), (0, ROWS - USED), constant_values=NEG)
    info = jnp.stack([logs, jnp.cos(rot), jnp.sin(rot)], axis=1)

    scores, stats, flipped = pl.pallas_call(
        score_kernel,
        out_shape=(
            jax.ShapeDtypeStruct((SHIFTS, ROWS, ROW_IMAGES), jnp.float32),
            jax.ShapeDtypeStruct((8, 8, LANES), jnp.float32),
            jax.ShapeDtypeStruct((2, SIDE, SIDE + 2 * MARGIN, LANES), jnp.float32),
        ),
        in_specs=[SMEM] + [VMEM] * 16,
        out_specs=(VMEM, VMEM, VMEM),
        scratch_shapes=[pltpu.VMEM((ROW_IMAGES, PIX + LANES), jnp.bfloat16)],
        compiler_params=PARAMS,
        name="scores",
    )(
        shift_table, images, a1, a2, c0, b1, b2, c1, c2, d1, d2, column, y1, y3, yw0, yw1, info
    )
    all_stats = lax.all_to_all(stats, AXES, 0, 0, axis_index_groups=X_ROWS)
    blocks, evidence = pl.pallas_call(
        sum_kernel,
        out_shape=(
            jax.ShapeDtypeStruct((BLOCKS, ROWS, LANES), jnp.bfloat16),
            jax.ShapeDtypeStruct((1, OWN), jnp.float32),
        ),
        in_specs=[SMEM] + [VMEM] * 4,
        out_specs=(VMEM, VMEM),
        scratch_shapes=[pltpu.VMEM((SHIFTS, ROWS, ROW_IMAGES), jnp.bfloat16)],
        compiler_params=PARAMS,
        name="sums",
    )(shift_table, scores, stats, all_stats, flipped)
    shares = lax.all_to_all(blocks, "img", 0, 0)
    sums, totals = pl.pallas_call(
        finish_kernel,
        out_shape=(
            jax.ShapeDtypeStruct((ROT, CLS, LANES), jnp.float32),
            jax.ShapeDtypeStruct((ROT, CLS), jnp.float32),
        ),
        in_specs=[VMEM],
        out_specs=(VMEM, VMEM),
        compiler_params=PARAMS,
        name="finish",
    )(shares)
    return jnp.transpose(sums, (1, 0, 2)), totals.T, evidence.reshape(OWN)


def solution(mesh):
    placed = (P(AXES, None), P(AXES), P("cls", None, "img"), P("cls"), P())
    return jax.shard_map(
        shards,
        mesh=mesh,
        in_specs=placed,
        out_specs=(P("cls", None, "img"), P("cls", None), P(AXES)),
        check_vma=False,
    )
```

```python
import math

import jax
import jax.numpy as jnp
from jax import lax
from jax.experimental import pallas as pl
from jax.experimental.pallas import tpu as pltpu
from jax.sharding import PartitionSpec as P

SCORE_GAIN = 2.5
PRIOR_WEIGHT = 1.0
AXES = ("cls", "img")
SIDE = 64
PIX = SIDE * SIDE
LANES = 128
BLOCKS = PIX // LANES
ROT = 12
HALF_ROT = ROT // 2
CLS = 25
USED = HALF_ROT * CLS
ROWS = 160
OWN = 32
ROW_IMAGES = 8 * OWN
SHIFTS = 11
MARGIN = 8
NEG = -1.0e30
UNROLL = 4
Z_ORDER = (0, -1, 1, 2)


def flat(x, core, z, y):
    x %= 4
    return ((x // 2) * 2 + core % 2) * 32 + (x % 2) * 16 + (z % 4) * 4 + y % 4


COORDS = [(x, c, z, y) for x in range(4) for c in range(2) for z in range(4) for y in range(4)]
X_ROWS = [[flat(x, c, z, y) for x in range(4) for c in range(2)] for z in range(4) for y in range(4)]


def move(value, x=0, core=0, z=0, y=0):
    route = [(flat(*a), flat(a[0] + x, a[1] + core, a[2] + z, a[3] + y)) for a in COORDS]
    return lax.ppermute(value, AXES, route)


def swap_x(value):
    route = [(flat(x, c, z, y), flat(x ^ 1, c, z, y)) for x, c, z, y in COORDS]
    return lax.ppermute(value, AXES, route)


def position():
    cls, img = lax.axis_index("cls"), lax.axis_index("img")
    x_lo, z, y = img // 16, (img // 4) % 4, img % 4
    return (cls // 2) * 2 + x_lo, cls % 2, x_lo, z, y


def shifted_pixels(t_ref, rows, dy, dx):
    parts = []
    for row in rows:
        at = jnp.bitwise_and(row + dy, SIDE - 1)
        tiles = [t_ref[t, at, pl.ds(MARGIN + dx, SIDE), :] for t in range(2)]
        parts.append(jnp.concatenate(tiles, axis=1).astype(jnp.bfloat16))
    return jnp.concatenate(parts, axis=0)


def prepare_kernel(*refs):
    sources, (keep_ref, give_ref, out_ref, info_ref) = refs[:4], refs[4:8]
    targets, half_ref, sems = refs[8:12], refs[12], refs[13]
    p_ref, x_ref, rot_ref, log_ref = targets
    _, _, x_lo, _, _ = position()
    copies = [
        pltpu.make_async_copy(sources[k], targets[k], sems.at[k]) for k in range(4)
    ]
    for copy in copies:
        copy.start()
    for copy in copies:
        copy.wait()
    for r in range(ROT):
        half, at = r // HALF_ROT, (r % HALF_ROT) * CLS
        half_ref[half, at : at + CLS, :] = p_ref[r].astype(jnp.float32)
    for half in range(2):
        half_ref[half, USED:ROWS, :] = jnp.zeros((ROWS - USED, LANES), jnp.float32)
    keep_ref[...] = half_ref[x_lo].astype(jnp.bfloat16)
    give_ref[...] = half_ref[1 - x_lo].astype(jnp.bfloat16)
    out_ref[:, 0:PIX] = x_ref[...].astype(jnp.bfloat16)
    rots = rot_ref[...].astype(jnp.float32)
    rots = jnp.concatenate([rots] * (LANES // OWN), axis=1)
    out_ref[:, PIX : PIX + LANES] = jnp.broadcast_to(rots, (OWN, LANES)).astype(jnp.bfloat16)
    diagonal = lax.broadcasted_iota(jnp.int32, (CLS, CLS), 0) == lax.broadcasted_iota(
        jnp.int32, (CLS, CLS), 1
    )
    logs = jnp.sum(jnp.where(diagonal, log_ref[...], 0.0), axis=1, keepdims=True)
    sign = (1 - 2 * x_lo).astype(jnp.float32)
    lane = lax.broadcasted_iota(jnp.int32, (CLS, LANES), 1)
    for r in range(HALF_ROT):
        turn = 2.0 * math.pi * r / ROT
        rows = jnp.where(lane == 1, math.cos(turn) * sign, math.sin(turn) * sign)
        info_ref[r * CLS : (r + 1) * CLS, :] = jnp.where(lane == 0, logs, rows)
    info_ref[USED:ROWS, :] = jnp.full((ROWS - USED, LANES), NEG, jnp.float32)


def turn_kernel(mine, other, t_ref, rot_ref, x_ref):
    x, core, _, _, _ = position()

    def put(value, dx, dc):
        slot = jnp.bitwise_and(x + dx, 3) * 2 + jnp.bitwise_xor(core, dc)
        x_ref[pl.ds(pl.multiple_of(slot * OWN, OWN), OWN), :] = value

    for k, dx in enumerate((0, -1, 1, 2)):
        put(mine[k * OWN : (k + 1) * OWN], dx, 0)
        put(other[k * OWN : (k + 1) * OWN], dx, 1)

    def turn_blocks(step, carry):
        for k in range(4):
            block = 4 * step + k
            lanes = pl.ds(pl.multiple_of(block * LANES, LANES), LANES)
            for t in range(2):
                tile = x_ref[pl.ds(t * LANES, LANES), lanes].astype(jnp.float32).T
                for half in range(2):
                    line = tile[half * SIDE : (half + 1) * SIDE]
                    t_ref[t, 2 * block + half, pl.ds(MARGIN, SIDE), :] = line
                    t_ref[t, 2 * block + half, pl.ds(0, MARGIN), :] = line[SIDE - MARGIN :]
                    t_ref[t, 2 * block + half, pl.ds(MARGIN + SIDE, MARGIN), :] = line[:MARGIN]
        return carry

    lax.fori_loop(0, BLOCKS // 4, turn_blocks, 0)
    lane_group = lax.broadcasted_iota(jnp.int32, (8, LANES), 1) // OWN
    for t in range(2):
        rots = jnp.zeros((8, LANES), jnp.float32)
        for k in range(4):
            start = t * LANES + k * OWN
            mine = x_ref[start : start + 16, PIX : PIX + LANES].astype(jnp.float32)[0:8]
            rots = jnp.where(lane_group == k, mine, rots)
        rot_ref[t] = rots


def add_scores(shift_ref, t_ref, pairs, s):
    _, _, x_lo, z, y = position()
    dy, dx = shift_ref[0, s], shift_ref[1, s]
    acc = jnp.zeros((ROWS, ROW_IMAGES), jnp.float32)
    for ref, at, dz, dyy in pairs:
        base = jnp.bitwise_and(z + dz, 3) * 4 + jnp.bitwise_and(y + dyy, 3)
        j0 = x_lo * 16 + base
        j1 = (1 - x_lo) * 16 + base
        moved = shifted_pixels(t_ref, (2 * j0, 2 * j0 + 1, 2 * j1, 2 * j1 + 1), dy, dx)
        panel = jnp.concatenate([ref[at], ref[at + 1]], axis=1)
        acc = acc + jnp.dot(panel, moved, preferred_element_type=jnp.float32)
    return acc


def squares_of(pairs):
    squares = jnp.zeros((ROWS, LANES), jnp.float32)
    for ref, at, _, _ in pairs:
        for k in range(2):
            value = ref[at + k].astype(jnp.float32)
            squares = squares + value * value
    return squares


def pairs_of(refs, offsets):
    return [
        (ref, 2 * i, dz, dy) for ref, dy in zip(refs, offsets) for i, dz in enumerate(Z_ORDER)
    ]


def first_kernel(shift_ref, t_ref, pc, py1, py3, s_ref, n_ref):
    pairs = pairs_of((pc, py1, py3), (0, -1, 1))
    n_ref[...] = squares_of(pairs)

    def one_shift(s, carry):
        s_ref[s] = add_scores(shift_ref, t_ref, pairs, s)
        return carry

    lax.fori_loop(0, SHIFTS, one_shift, 0, unroll=True)


def last_kernel(shift_ref, t_ref, py2, s_in, n_in, rot_ref, info_ref, e_ref, st_ref):
    gain = SCORE_GAIN / math.sqrt(PIX)
    pairs = pairs_of((py2,), (2,))
    norms = jnp.sum(n_in[...] + squares_of(pairs), axis=1, keepdims=True)
    rots = jnp.concatenate([rot_ref[0], rot_ref[1]], axis=1)
    angle = rots[0:1] * (2.0 * math.pi / ROT)
    info = info_ref[...]
    prior = info[:, 1:2] * jnp.cos(angle) + info[:, 2:3] * jnp.sin(angle)
    bias = info[:, 0:1] - 0.5 * gain * norms + PRIOR_WEIGHT * prior
    is_panel = lax.broadcasted_iota(jnp.int32, (ROWS, 1), 0) < USED
    bias = jnp.where(is_panel, bias, NEG)

    def one_shift(s, peak):
        scores = gain * (s_in[s] + add_scores(shift_ref, t_ref, pairs, s)) + bias
        e_ref[s] = scores
        return jnp.maximum(peak, jnp.max(scores, axis=0, keepdims=True))

    peak = lax.fori_loop(
        0, SHIFTS, one_shift, jnp.full((1, ROW_IMAGES), NEG, jnp.float32), unroll=True
    )

    def one_exp(s, total):
        value = jnp.exp(e_ref[s] - peak)
        e_ref[s] = value
        return total + jnp.sum(value, axis=0, keepdims=True)

    total = lax.fori_loop(
        0, SHIFTS, one_exp, jnp.zeros((1, ROW_IMAGES), jnp.float32), unroll=True
    )
    stats = jnp.concatenate(
        [
            peak[:, :LANES],
            peak[:, LANES:],
            total[:, :LANES],
            total[:, LANES:],
            jnp.zeros((4, LANES), jnp.float32),
        ],
        axis=0,
    )
    for k in range(8):
        st_ref[k] = stats


def sum_kernel(shift_ref, e_ref, st_ref, all_ref, t_ref, out_ref, ev_ref, w_ref):
    x, core, _, _, _ = position()
    stats = [all_ref[k] for k in range(8)]
    peak = stats[0][0:2]
    for k in range(1, 8):
        peak = jnp.maximum(peak, stats[k][0:2])
    total = jnp.zeros((2, LANES), jnp.float32)
    for k in range(8):
        total = total + stats[k][2:4] * jnp.exp(stats[k][0:2] - peak)
    evidence = peak + jnp.log(total)
    slot = x * 2 + core
    mine = jnp.where(slot >= 4, evidence[1:2], evidence[0:1])
    groups = [mine[:, k * OWN : (k + 1) * OWN] for k in range(4)]
    at = jnp.bitwise_and(slot, 3)
    picked = groups[0]
    for k in range(1, 4):
        picked = jnp.where(at == k, groups[k], picked)
    ev_ref[...] = picked
    factor = jnp.exp(st_ref[0][0:2] - peak) / total
    factor = jnp.concatenate([factor[0:1], factor[1:2]], axis=1)

    for s in range(SHIFTS):
        weight = (e_ref[s] * factor).astype(jnp.bfloat16)
        w_ref[s * ROW_IMAGES : (s + 1) * ROW_IMAGES, :] = weight.T

    ones = jnp.ones((16, SHIFTS * ROW_IMAGES), jnp.bfloat16)
    totals = jnp.dot(ones, w_ref[...], preferred_element_type=jnp.float32)[0:1]
    totals = jnp.concatenate([totals, jnp.zeros((1, 2 * LANES - ROWS), jnp.float32)], axis=1)
    pieces = []
    for _ in range(3):
        part = totals.astype(jnp.bfloat16).astype(jnp.float32)
        totals = totals - part
        pieces += [part[:, :LANES], part[:, LANES:]]
    tail = jnp.concatenate(
        [jnp.zeros((6, LANES), jnp.float32)] + pieces + [jnp.zeros((4, LANES), jnp.float32)], axis=0
    ).astype(jnp.bfloat16)
    is_tail = lax.broadcasted_iota(jnp.int32, (16, LANES), 0) >= 6

    def one_block(pair, carry):
        rows = tuple(4 * pair + k for k in range(4))
        moved = jnp.concatenate(
            [
                shifted_pixels(t_ref, rows, shift_ref[0, s], shift_ref[1, s])
                for s in range(SHIFTS)
            ],
            axis=1,
        )
        acc = jnp.dot(moved, w_ref[...], preferred_element_type=jnp.float32)
        turned = acc.astype(jnp.bfloat16).T
        for k in range(2):
            part = turned[:, k * LANES : (k + 1) * LANES]
            out_ref[2 * pair + k, 0 : ROWS - 16, :] = part[: ROWS - 16]
            out_ref[2 * pair + k, ROWS - 16 : ROWS, :] = jnp.where(is_tail, tail, part[ROWS - 16 :])
        return carry

    lax.fori_loop(0, BLOCKS // 2, one_block, 0, unroll=UNROLL)


def finish_kernel(in_ref, out_ref, wt_ref):
    for half in range(2):
        acc = jnp.zeros((ROWS, LANES), jnp.float32)
        for k in range(16):
            acc = acc + in_ref[half * 16 + k].astype(jnp.float32)
        for r in range(HALF_ROT):
            out_ref[half * HALF_ROT + r] = acc[r * CLS : (r + 1) * CLS]
        wide = [
            acc[USED + k : USED + k + 1] + acc[USED + 2 + k : USED + 3 + k]
            + acc[USED + 4 + k : USED + 5 + k]
            for k in range(2)
        ]
        totals = jnp.concatenate(wide, axis=1)
        for r in range(HALF_ROT):
            row = half * HALF_ROT + r
            wt_ref[row : row + 1, :] = totals[:, r * CLS : (r + 1) * CLS]


VMEM = pl.BlockSpec(memory_space=pltpu.VMEM)
SMEM = pl.BlockSpec(memory_space=pltpu.SMEM)
PARAMS = pltpu.CompilerParams(vmem_limit_bytes=40 * 1024 * 1024)


def cost(quarters, megabytes):
    flops = 1000 * quarters
    return pl.CostEstimate(flops=flops, bytes_accessed=1000 * megabytes, transcendentals=0)


def shards(particles, rot_prior, panels, log_prior, shift_table):
    x_lo = lax.axis_index("img") // 16

    keep, give, images, info = pl.pallas_call(
        prepare_kernel,
        out_shape=(jax.ShapeDtypeStruct((ROWS, LANES), jnp.bfloat16),) * 2
        + (
            jax.ShapeDtypeStruct((OWN, PIX + LANES), jnp.bfloat16),
            jax.ShapeDtypeStruct((ROWS, LANES), jnp.float32),
        ),
        in_specs=[pl.BlockSpec(memory_space=pltpu.HBM)] * 4,
        out_specs=(VMEM,) * 4,
        scratch_shapes=[
            pltpu.VMEM((ROT, CLS, LANES), jnp.bfloat16),
            pltpu.VMEM((OWN, PIX), jnp.float32),
            pltpu.VMEM((1, OWN), jnp.int32),
            pltpu.VMEM((1, CLS), jnp.float32),
            pltpu.VMEM((2, ROWS, LANES), jnp.float32),
            pltpu.SemaphoreType.DMA((4,)),
        ],
        compiler_params=pltpu.CompilerParams(vmem_limit_bytes=60 * 1024 * 1024),
        cost_estimate=cost(0, 1),
        name="prepare",
    )(
        jnp.transpose(panels, (1, 0, 2)),
        particles,
        rot_prior.reshape(1, OWN),
        log_prior.reshape(1, CLS),
    )
    got = swap_x(give)
    first = jnp.stack([keep, got])
    z1 = move(first, z=1)
    z3 = move(first, z=-1)
    z2 = move(first, z=2)
    images, _ = lax.optimization_barrier((images, got))
    a1 = move(images, x=1)
    a2 = move(images, x=-1)
    a3 = move(images, x=2)
    column = jnp.concatenate([first, z1, z3, z2], axis=0)
    y1 = move(column, y=1)
    y3 = move(column, y=-1)
    y2 = move(column, y=2)
    mine = jnp.concatenate([images, a1, a2, a3], axis=0)
    mine, y1, y3 = lax.optimization_barrier((mine, y1, y3))
    cc = move(mine, core=1)

    turned, rots = pl.pallas_call(
        turn_kernel,
        out_shape=(
            jax.ShapeDtypeStruct((2, SIDE, SIDE + 2 * MARGIN, LANES), jnp.float32),
            jax.ShapeDtypeStruct((2, 8, LANES), jnp.float32),
        ),
        in_specs=[VMEM] * 2,
        out_specs=(VMEM, VMEM),
        scratch_shapes=[pltpu.VMEM((ROW_IMAGES, PIX + LANES), jnp.bfloat16)],
        compiler_params=PARAMS,
        cost_estimate=cost(0, 8),
        name="turn",
    )(mine, cc)

    shifts = shift_table.T
    score_shape = jax.ShapeDtypeStruct((SHIFTS, ROWS, ROW_IMAGES), jnp.float32)
    norm_shape = jax.ShapeDtypeStruct((ROWS, LANES), jnp.float32)
    scores, norms = pl.pallas_call(
        first_kernel,
        out_shape=(score_shape, norm_shape),
        in_specs=[SMEM] + [VMEM] * 4,
        out_specs=(VMEM, VMEM),
        compiler_params=PARAMS,
        cost_estimate=cost(3, 4),
        name="first",
    )(shifts, turned, column, y1, y3)

    scores, stats = pl.pallas_call(
        last_kernel,
        out_shape=(score_shape, jax.ShapeDtypeStruct((8, 8, LANES), jnp.float32)),
        in_specs=[SMEM] + [VMEM] * 6,
        out_specs=(VMEM, VMEM),
        input_output_aliases={3: 0},
        compiler_params=PARAMS,
        cost_estimate=cost(1, 8),
        name="last",
    )(shifts, turned, y2, scores, norms, rots, info)
    all_stats = lax.all_to_all(stats, AXES, 0, 0, axis_index_groups=X_ROWS)
    blocks, evidence = pl.pallas_call(
        sum_kernel,
        out_shape=(
            jax.ShapeDtypeStruct((BLOCKS, ROWS, LANES), jnp.bfloat16),
            jax.ShapeDtypeStruct((1, OWN), jnp.float32),
        ),
        in_specs=[SMEM] + [VMEM] * 4,
        out_specs=(VMEM, VMEM),
        scratch_shapes=[pltpu.VMEM((SHIFTS * ROW_IMAGES, ROWS), jnp.bfloat16)],
        compiler_params=PARAMS,
        cost_estimate=cost(4, 12),
        name="sums",
    )(shifts, scores, stats, all_stats, turned)
    shares = lax.all_to_all(blocks, "img", 0, 0)
    sums, totals = pl.pallas_call(
        finish_kernel,
        out_shape=(
            jax.ShapeDtypeStruct((ROT, CLS, LANES), jnp.float32),
            jax.ShapeDtypeStruct((ROT, CLS), jnp.float32),
        ),
        in_specs=[VMEM],
        out_specs=(VMEM, VMEM),
        compiler_params=PARAMS,
        name="finish",
    )(shares)
    return jnp.transpose(sums, (1, 0, 2)), totals.T, evidence.reshape(OWN)


def solution(mesh):
    placed = (P(AXES, None), P(AXES), P("cls", None, "img"), P("cls"), P())
    return jax.shard_map(
        shards,
        mesh=mesh,
        in_specs=placed,
        out_specs=(P("cls", None, "img"), P("cls", None), P(AXES)),
        check_vma=False,
    )
```

```python
import math

import jax
import jax.numpy as jnp
from jax import lax
from jax.experimental import pallas as pl
from jax.experimental.pallas import tpu as pltpu
from jax.sharding import PartitionSpec as P

SCORE_GAIN = 2.5
PRIOR_WEIGHT = 1.0
AXES = ("cls", "img")
SIDE = 64
PIX = SIDE * SIDE
LANES = 128
BLOCKS = PIX // LANES
ROT = 12
HALF_ROT = ROT // 2
CLS = 25
USED = HALF_ROT * CLS
ROWS = 160
OWN = 32
ROW_IMAGES = 8 * OWN
SHIFTS = 11
MARGIN = 8
NEG = -1.0e30
UNROLL = 4


def flat(x, core, z, y):
    x %= 4
    return ((x // 2) * 2 + core % 2) * 32 + (x % 2) * 16 + (z % 4) * 4 + y % 4


COORDS = [(x, c, z, y) for x in range(4) for c in range(2) for z in range(4) for y in range(4)]
XZ_GROUPS = [[x * 16 + z * 4 + y for x in range(2) for z in range(4)] for y in range(4)]
X_ROWS = [[flat(x, c, z, y) for x in range(4) for c in range(2)] for z in range(4) for y in range(4)]


def move(value, x=0, core=0, z=0, y=0):
    route = [(flat(*a), flat(a[0] + x, a[1] + core, a[2] + z, a[3] + y)) for a in COORDS]
    return lax.ppermute(value, AXES, route)


def position():
    cls, img = lax.axis_index("cls"), lax.axis_index("img")
    x_lo, z, y = img // 16, (img // 4) % 4, img % 4
    return (cls // 2) * 2 + x_lo, cls % 2, x_lo, z, y


def shifted_pixels(t_ref, rows, dy, dx):
    parts = []
    for row in rows:
        at = jnp.bitwise_and(row + dy, SIDE - 1)
        tiles = [t_ref[t, at, pl.ds(MARGIN + dx, SIDE), :] for t in range(2)]
        parts.append(jnp.concatenate(tiles, axis=1).astype(jnp.bfloat16))
    return jnp.concatenate(parts, axis=0)


def prepare_kernel(*refs):
    sources, (send_ref, out_ref, info_ref) = refs[:4], refs[4:7]
    targets, half_ref, sems = refs[7:11], refs[11], refs[12]
    p_ref, x_ref, rot_ref, log_ref = targets
    _, _, x_lo, _, _ = position()
    copies = [
        pltpu.make_async_copy(sources[k], targets[k], sems.at[k]) for k in range(4)
    ]
    for copy in copies:
        copy.start()
    for copy in copies:
        copy.wait()
    for r in range(ROT):
        half, at = r // HALF_ROT, (r % HALF_ROT) * CLS
        half_ref[half, at : at + CLS, :] = p_ref[r].astype(jnp.float32)
    for half in range(2):
        half_ref[half, USED:ROWS, :] = jnp.zeros((ROWS - USED, LANES), jnp.float32)
    for half in range(2):
        value = half_ref[half].astype(jnp.bfloat16)
        for k in range(4):
            send_ref[4 * half + k] = value
    out_ref[:, 0:PIX] = x_ref[...].astype(jnp.bfloat16)
    rots = rot_ref[...].astype(jnp.float32)
    rots = jnp.concatenate([rots] * (LANES // OWN), axis=1)
    out_ref[:, PIX : PIX + LANES] = jnp.broadcast_to(rots, (OWN, LANES)).astype(jnp.bfloat16)
    diagonal = lax.broadcasted_iota(jnp.int32, (CLS, CLS), 0) == lax.broadcasted_iota(
        jnp.int32, (CLS, CLS), 1
    )
    logs = jnp.sum(jnp.where(diagonal, log_ref[...], 0.0), axis=1, keepdims=True)
    sign = (1 - 2 * x_lo).astype(jnp.float32)
    lane = lax.broadcasted_iota(jnp.int32, (CLS, LANES), 1)
    for r in range(HALF_ROT):
        turn = 2.0 * math.pi * r / ROT
        rows = jnp.where(lane == 1, math.cos(turn) * sign, math.sin(turn) * sign)
        info_ref[r * CLS : (r + 1) * CLS, :] = jnp.where(lane == 0, logs, rows)
    info_ref[USED:ROWS, :] = jnp.full((ROWS - USED, LANES), NEG, jnp.float32)


def turn_kernel(mine, other, t_ref, rot_ref, x_ref):
    x, core, _, _, _ = position()

    def put(value, dx, dc):
        slot = jnp.bitwise_and(x + dx, 3) * 2 + jnp.bitwise_xor(core, dc)
        x_ref[pl.ds(pl.multiple_of(slot * OWN, OWN), OWN), :] = value

    for k, dx in enumerate((0, -1, 1, 2)):
        put(mine[k * OWN : (k + 1) * OWN], dx, 0)
        put(other[k * OWN : (k + 1) * OWN], dx, 1)

    def turn_blocks(step, carry):
        for k in range(4):
            block = 4 * step + k
            lanes = pl.ds(pl.multiple_of(block * LANES, LANES), LANES)
            for t in range(2):
                tile = x_ref[pl.ds(t * LANES, LANES), lanes].astype(jnp.float32).T
                for half in range(2):
                    line = tile[half * SIDE : (half + 1) * SIDE]
                    t_ref[t, 2 * block + half, pl.ds(MARGIN, SIDE), :] = line
                    t_ref[t, 2 * block + half, pl.ds(0, MARGIN), :] = line[SIDE - MARGIN :]
                    t_ref[t, 2 * block + half, pl.ds(MARGIN + SIDE, MARGIN), :] = line[:MARGIN]
        return carry

    lax.fori_loop(0, BLOCKS // 4, turn_blocks, 0)
    lane_group = lax.broadcasted_iota(jnp.int32, (8, LANES), 1) // OWN
    for t in range(2):
        rots = jnp.zeros((8, LANES), jnp.float32)
        for k in range(4):
            start = t * LANES + k * OWN
            mine = x_ref[start : start + 16, PIX : PIX + LANES].astype(jnp.float32)[0:8]
            rots = jnp.where(lane_group == k, mine, rots)
        rot_ref[t] = rots


def add_scores(shift_ref, t_ref, pairs, s):
    y = position()[4]
    dy, dx = shift_ref[0, s], shift_ref[1, s]
    acc = jnp.zeros((ROWS, ROW_IMAGES), jnp.float32)
    for low, high, z, dyy in pairs:
        j0 = z * 4 + jnp.bitwise_and(y + dyy, 3)
        j1 = j0 + 16
        moved = shifted_pixels(t_ref, (2 * j0, 2 * j0 + 1, 2 * j1, 2 * j1 + 1), dy, dx)
        panel = jnp.concatenate([low[z], high[z]], axis=1)
        acc = acc + jnp.dot(panel, moved, preferred_element_type=jnp.float32)
    return acc


def squares_of(pairs):
    squares = jnp.zeros((ROWS, LANES), jnp.float32)
    for low, high, z, _ in pairs:
        for ref in (low, high):
            value = ref[z].astype(jnp.float32)
            squares = squares + value * value
    return squares


def pairs_of(refs, offsets):
    return [(*ref, z, dy) for ref, dy in zip(refs, offsets) for z in range(4)]


def halves(ref):
    return ref.at[0:4], ref.at[4:8]


def first_kernel(shift_ref, t_ref, pc, py1, py3, s_ref, n_ref):
    pairs = pairs_of((halves(pc), halves(py1), halves(py3)), (0, -1, 1))
    n_ref[...] = squares_of(pairs)

    def one_shift(s, carry):
        s_ref[s] = add_scores(shift_ref, t_ref, pairs, s)
        return carry

    lax.fori_loop(0, SHIFTS, one_shift, 0, unroll=True)


def last_kernel(shift_ref, t_ref, pw0, pw1, s_in, n_in, rot_ref, info_ref, e_ref, st_ref):
    gain = SCORE_GAIN / math.sqrt(PIX)
    pairs = pairs_of(((pw0, pw1),), (2,))
    norms = jnp.sum(n_in[...] + squares_of(pairs), axis=1, keepdims=True)
    rots = jnp.concatenate([rot_ref[0], rot_ref[1]], axis=1)
    angle = rots[0:1] * (2.0 * math.pi / ROT)
    info = info_ref[...]
    prior = info[:, 1:2] * jnp.cos(angle) + info[:, 2:3] * jnp.sin(angle)
    bias = info[:, 0:1] - 0.5 * gain * norms + PRIOR_WEIGHT * prior
    is_panel = lax.broadcasted_iota(jnp.int32, (ROWS, 1), 0) < USED
    bias = jnp.where(is_panel, bias, NEG)

    def one_shift(s, peak):
        scores = gain * (s_in[s] + add_scores(shift_ref, t_ref, pairs, s)) + bias
        e_ref[s] = scores
        return jnp.maximum(peak, jnp.max(scores, axis=0, keepdims=True))

    peak = lax.fori_loop(
        0, SHIFTS, one_shift, jnp.full((1, ROW_IMAGES), NEG, jnp.float32), unroll=True
    )

    def one_exp(s, total):
        value = jnp.exp(e_ref[s] - peak)
        e_ref[s] = value
        return total + jnp.sum(value, axis=0, keepdims=True)

    total = lax.fori_loop(
        0, SHIFTS, one_exp, jnp.zeros((1, ROW_IMAGES), jnp.float32), unroll=True
    )
    stats = jnp.concatenate(
        [
            peak[:, :LANES],
            peak[:, LANES:],
            total[:, :LANES],
            total[:, LANES:],
            jnp.zeros((4, LANES), jnp.float32),
        ],
        axis=0,
    )
    for k in range(8):
        st_ref[k] = stats


def sum_kernel(shift_ref, e_ref, st_ref, all_ref, t_ref, out_ref, ev_ref, w_ref):
    x, core, _, _, _ = position()
    stats = [all_ref[k] for k in range(8)]
    peak = stats[0][0:2]
    for k in range(1, 8):
        peak = jnp.maximum(peak, stats[k][0:2])
    total = jnp.zeros((2, LANES), jnp.float32)
    for k in range(8):
        total = total + stats[k][2:4] * jnp.exp(stats[k][0:2] - peak)
    evidence = peak + jnp.log(total)
    slot = x * 2 + core
    mine = jnp.where(slot >= 4, evidence[1:2], evidence[0:1])
    groups = [mine[:, k * OWN : (k + 1) * OWN] for k in range(4)]
    at = jnp.bitwise_and(slot, 3)
    picked = groups[0]
    for k in range(1, 4):
        picked = jnp.where(at == k, groups[k], picked)
    ev_ref[...] = picked
    factor = jnp.exp(st_ref[0][0:2] - peak) / total
    factor = jnp.concatenate([factor[0:1], factor[1:2]], axis=1)

    for s in range(SHIFTS):
        weight = (e_ref[s] * factor).astype(jnp.bfloat16)
        w_ref[s * ROW_IMAGES : (s + 1) * ROW_IMAGES, :] = weight.T

    ones = jnp.ones((16, SHIFTS * ROW_IMAGES), jnp.bfloat16)
    totals = jnp.dot(ones, w_ref[...], preferred_element_type=jnp.float32)[0:1]
    totals = jnp.concatenate([totals, jnp.zeros((1, 2 * LANES - ROWS), jnp.float32)], axis=1)
    pieces = []
    for _ in range(3):
        part = totals.astype(jnp.bfloat16).astype(jnp.float32)
        totals = totals - part
        pieces += [part[:, :LANES], part[:, LANES:]]
    tail = jnp.concatenate(
        [jnp.zeros((6, LANES), jnp.float32)] + pieces + [jnp.zeros((4, LANES), jnp.float32)], axis=0
    ).astype(jnp.bfloat16)
    is_tail = lax.broadcasted_iota(jnp.int32, (16, LANES), 0) >= 6

    def one_block(pair, carry):
        rows = tuple(4 * pair + k for k in range(4))
        moved = jnp.concatenate(
            [
                shifted_pixels(t_ref, rows, shift_ref[0, s], shift_ref[1, s])
                for s in range(SHIFTS)
            ],
            axis=1,
        )
        acc = jnp.dot(moved, w_ref[...], preferred_element_type=jnp.float32)
        turned = acc.astype(jnp.bfloat16).T
        for k in range(2):
            part = turned[:, k * LANES : (k + 1) * LANES]
            out_ref[2 * pair + k, 0 : ROWS - 16, :] = part[: ROWS - 16]
            out_ref[2 * pair + k, ROWS - 16 : ROWS, :] = jnp.where(is_tail, tail, part[ROWS - 16 :])
        return carry

    lax.fori_loop(0, BLOCKS // 2, one_block, 0, unroll=UNROLL)


def finish_kernel(in_ref, out_ref, wt_ref):
    for half in range(2):
        acc = jnp.zeros((ROWS, LANES), jnp.float32)
        for k in range(16):
            acc = acc + in_ref[half * 16 + k].astype(jnp.float32)
        for r in range(HALF_ROT):
            out_ref[half * HALF_ROT + r] = acc[r * CLS : (r + 1) * CLS]
        wide = [
            acc[USED + k : USED + k + 1] + acc[USED + 2 + k : USED + 3 + k]
            + acc[USED + 4 + k : USED + 5 + k]
            for k in range(2)
        ]
        totals = jnp.concatenate(wide, axis=1)
        for r in range(HALF_ROT):
            row = half * HALF_ROT + r
            wt_ref[row : row + 1, :] = totals[:, r * CLS : (r + 1) * CLS]


VMEM = pl.BlockSpec(memory_space=pltpu.VMEM)
SMEM = pl.BlockSpec(memory_space=pltpu.SMEM)
PARAMS = pltpu.CompilerParams(vmem_limit_bytes=40 * 1024 * 1024)


def cost(quarters, megabytes):
    flops = 1000 * quarters
    return pl.CostEstimate(flops=flops, bytes_accessed=1000 * megabytes, transcendentals=0)


def shards(particles, rot_prior, panels, log_prior, shift_table):
    spread, images, info = pl.pallas_call(
        prepare_kernel,
        out_shape=(
            jax.ShapeDtypeStruct((8, ROWS, LANES), jnp.bfloat16),
            jax.ShapeDtypeStruct((OWN, PIX + LANES), jnp.bfloat16),
            jax.ShapeDtypeStruct((ROWS, LANES), jnp.float32),
        ),
        in_specs=[pl.BlockSpec(memory_space=pltpu.HBM)] * 4,
        out_specs=(VMEM,) * 3,
        scratch_shapes=[
            pltpu.VMEM((ROT, CLS, LANES), jnp.bfloat16),
            pltpu.VMEM((OWN, PIX), jnp.float32),
            pltpu.VMEM((1, OWN), jnp.int32),
            pltpu.VMEM((1, CLS), jnp.float32),
            pltpu.VMEM((2, ROWS, LANES), jnp.float32),
            pltpu.SemaphoreType.DMA((4,)),
        ],
        compiler_params=pltpu.CompilerParams(vmem_limit_bytes=60 * 1024 * 1024),
        cost_estimate=cost(0, 1),
        name="prepare",
    )(
        jnp.transpose(panels, (1, 0, 2)),
        particles,
        rot_prior.reshape(1, OWN),
        log_prior.reshape(1, CLS),
    )
    a1 = move(images, x=1)
    a2 = move(images, x=-1)
    a3 = move(images, x=2)
    column = lax.all_to_all(spread, "img", 0, 0, axis_index_groups=XZ_GROUPS)
    y1 = move(column, y=1)
    y3 = move(column, y=-1)
    mine = jnp.concatenate([images, a1, a2, a3], axis=0)
    mine, y1, y3 = lax.optimization_barrier((mine, y1, y3))
    cc = move(mine, core=1)
    yw0 = move(y1[:4], y=1)
    yw1 = move(y3[4:], y=-1)

    turned, rots = pl.pallas_call(
        turn_kernel,
        out_shape=(
            jax.ShapeDtypeStruct((2, SIDE, SIDE + 2 * MARGIN, LANES), jnp.float32),
            jax.ShapeDtypeStruct((2, 8, LANES), jnp.float32),
        ),
        in_specs=[VMEM] * 2,
        out_specs=(VMEM, VMEM),
        scratch_shapes=[pltpu.VMEM((ROW_IMAGES, PIX + LANES), jnp.bfloat16)],
        compiler_params=PARAMS,
        cost_estimate=cost(0, 8),
        name="turn",
    )(mine, cc)

    shifts = shift_table.T
    score_shape = jax.ShapeDtypeStruct((SHIFTS, ROWS, ROW_IMAGES), jnp.float32)
    norm_shape = jax.ShapeDtypeStruct((ROWS, LANES), jnp.float32)
    scores, norms = pl.pallas_call(
        first_kernel,
        out_shape=(score_shape, norm_shape),
        in_specs=[SMEM] + [VMEM] * 4,
        out_specs=(VMEM, VMEM),
        compiler_params=PARAMS,
        cost_estimate=cost(3, 4),
        name="first",
    )(shifts, turned, column, y1, y3)

    scores, stats = pl.pallas_call(
        last_kernel,
        out_shape=(score_shape, jax.ShapeDtypeStruct((8, 8, LANES), jnp.float32)),
        in_specs=[SMEM] + [VMEM] * 7,
        out_specs=(VMEM, VMEM),
        input_output_aliases={4: 0},
        compiler_params=PARAMS,
        cost_estimate=cost(1, 8),
        name="last",
    )(shifts, turned, yw0, yw1, scores, norms, rots, info)
    all_stats = lax.all_to_all(stats, AXES, 0, 0, axis_index_groups=X_ROWS)
    blocks, evidence = pl.pallas_call(
        sum_kernel,
        out_shape=(
            jax.ShapeDtypeStruct((BLOCKS, ROWS, LANES), jnp.bfloat16),
            jax.ShapeDtypeStruct((1, OWN), jnp.float32),
        ),
        in_specs=[SMEM] + [VMEM] * 4,
        out_specs=(VMEM, VMEM),
        scratch_shapes=[pltpu.VMEM((SHIFTS * ROW_IMAGES, ROWS), jnp.bfloat16)],
        compiler_params=PARAMS,
        cost_estimate=cost(4, 12),
        name="sums",
    )(shifts, scores, stats, all_stats, turned)
    shares = lax.all_to_all(blocks, "img", 0, 0)
    sums, totals = pl.pallas_call(
        finish_kernel,
        out_shape=(
            jax.ShapeDtypeStruct((ROT, CLS, LANES), jnp.float32),
            jax.ShapeDtypeStruct((ROT, CLS), jnp.float32),
        ),
        in_specs=[VMEM],
        out_specs=(VMEM, VMEM),
        compiler_params=PARAMS,
        name="finish",
    )(shares)
    return jnp.transpose(sums, (1, 0, 2)), totals.T, evidence.reshape(OWN)


def solution(mesh):
    placed = (P(AXES, None), P(AXES), P("cls", None, "img"), P("cls"), P())
    return jax.shard_map(
        shards,
        mesh=mesh,
        in_specs=placed,
        out_specs=(P("cls", None, "img"), P("cls", None), P(AXES)),
        check_vma=False,
    )
```

```python
import math

import jax
import jax.numpy as jnp
from jax import lax
from jax.experimental import pallas as pl
from jax.experimental.pallas import tpu as pltpu
from jax.sharding import PartitionSpec as P

SCORE_GAIN = 2.5
PRIOR_WEIGHT = 1.0
AXES = ("cls", "img")
SIDE = 64
PIX = SIDE * SIDE
LANES = 128
BLOCKS = PIX // LANES
ROT = 12
HALF_ROT = ROT // 2
CLS = 25
USED = HALF_ROT * CLS
ROWS = 160
OWN = 32
ROW_IMAGES = 8 * OWN
SHIFTS = 11
MARGIN = 8
NEG = -1.0e30


def flat(x, core, z, y):
    x %= 4
    return ((x // 2) * 2 + core % 2) * 32 + (x % 2) * 16 + (z % 4) * 4 + y % 4


COORDS = [(x, c, z, y) for x in range(4) for c in range(2) for z in range(4) for y in range(4)]
XZ_GROUPS = [[x * 16 + z * 4 + y for x in range(2) for z in range(4)] for y in range(4)]
X_ROWS = [[flat(x, c, z, y) for x in range(4) for c in range(2)] for z in range(4) for y in range(4)]


def move(value, x=0, core=0, z=0, y=0):
    route = [(flat(*a), flat(a[0] + x, a[1] + core, a[2] + z, a[3] + y)) for a in COORDS]
    return lax.ppermute(value, AXES, route)


def position():
    cls, img = lax.axis_index("cls"), lax.axis_index("img")
    x_lo, z, y = img // 16, (img // 4) % 4, img % 4
    return (cls // 2) * 2 + x_lo, cls % 2, x_lo, z, y


def shifted_pixels(t_ref, rows, dy, dx):
    parts = []
    for row in rows:
        at = jnp.bitwise_and(row + dy, SIDE - 1)
        tiles = [t_ref[t, at, pl.ds(MARGIN + dx, SIDE), :] for t in range(2)]
        parts.append(jnp.concatenate(tiles, axis=1).astype(jnp.bfloat16))
    return jnp.concatenate(parts, axis=0)


def prepare_kernel(*refs):
    sources, (send_ref, out_ref, info_ref) = refs[:4], refs[4:7]
    targets, half_ref, sems = refs[7:11], refs[11], refs[12]
    p_ref, x_ref, rot_ref, log_ref = targets
    _, _, x_lo, _, _ = position()
    copies = [
        pltpu.make_async_copy(sources[k], targets[k], sems.at[k]) for k in range(4)
    ]
    for copy in copies:
        copy.start()
    for copy in copies:
        copy.wait()
    for r in range(ROT):
        half, at = r // HALF_ROT, (r % HALF_ROT) * CLS
        half_ref[half, at : at + CLS, :] = p_ref[r].astype(jnp.float32)
    for half in range(2):
        half_ref[half, USED:ROWS, :] = jnp.zeros((ROWS - USED, LANES), jnp.float32)
    for half in range(2):
        value = half_ref[half].astype(jnp.bfloat16)
        for k in range(4):
            send_ref[4 * half + k] = value
    out_ref[:, 0:PIX] = x_ref[...].astype(jnp.bfloat16)
    rots = rot_ref[...].astype(jnp.float32)
    rots = jnp.concatenate([rots] * (LANES // OWN), axis=1)
    out_ref[:, PIX : PIX + LANES] = jnp.broadcast_to(rots, (OWN, LANES)).astype(jnp.bfloat16)
    diagonal = lax.broadcasted_iota(jnp.int32, (CLS, CLS), 0) == lax.broadcasted_iota(
        jnp.int32, (CLS, CLS), 1
    )
    logs = jnp.sum(jnp.where(diagonal, log_ref[...], 0.0), axis=1, keepdims=True)
    sign = (1 - 2 * x_lo).astype(jnp.float32)
    lane = lax.broadcasted_iota(jnp.int32, (CLS, LANES), 1)
    for r in range(HALF_ROT):
        turn = 2.0 * math.pi * r / ROT
        rows = jnp.where(lane == 1, math.cos(turn) * sign, math.sin(turn) * sign)
        info_ref[r * CLS : (r + 1) * CLS, :] = jnp.where(lane == 0, logs, rows)
    info_ref[USED:ROWS, :] = jnp.full((ROWS - USED, LANES), NEG, jnp.float32)


def turn_kernel(mine, other, t_ref, rot_ref, x_ref):
    x, core, _, _, _ = position()

    def put(value, dx, dc):
        slot = jnp.bitwise_and(x + dx, 3) * 2 + jnp.bitwise_xor(core, dc)
        x_ref[pl.ds(pl.multiple_of(slot * OWN, OWN), OWN), :] = value

    for k, dx in enumerate((0, -1, 1, 2)):
        put(mine[k * OWN : (k + 1) * OWN], dx, 0)
        put(other[k * OWN : (k + 1) * OWN], dx, 1)

    def turn_blocks(step, carry):
        for k in range(4):
            block = 4 * step + k
            lanes = pl.ds(pl.multiple_of(block * LANES, LANES), LANES)
            for t in range(2):
                tile = x_ref[pl.ds(t * LANES, LANES), lanes].astype(jnp.float32).T
                for half in range(2):
                    line = tile[half * SIDE : (half + 1) * SIDE]
                    t_ref[t, 2 * block + half, pl.ds(MARGIN, SIDE), :] = line
                    t_ref[t, 2 * block + half, pl.ds(0, MARGIN), :] = line[SIDE - MARGIN :]
                    t_ref[t, 2 * block + half, pl.ds(MARGIN + SIDE, MARGIN), :] = line[:MARGIN]
        return carry

    lax.fori_loop(0, BLOCKS // 4, turn_blocks, 0)
    lane_group = lax.broadcasted_iota(jnp.int32, (8, LANES), 1) // OWN
    for t in range(2):
        rots = jnp.zeros((8, LANES), jnp.float32)
        for k in range(4):
            start = t * LANES + k * OWN
            mine = x_ref[start : start + 16, PIX : PIX + LANES].astype(jnp.float32)[0:8]
            rots = jnp.where(lane_group == k, mine, rots)
        rot_ref[t] = rots


def add_scores(shift_ref, t_ref, pairs, s):
    y = position()[4]
    dy, dx = shift_ref[0, s], shift_ref[1, s]
    acc = jnp.zeros((ROWS, ROW_IMAGES), jnp.float32)
    for low, high, z, dyy in pairs:
        j0 = z * 4 + jnp.bitwise_and(y + dyy, 3)
        j1 = j0 + 16
        moved = shifted_pixels(t_ref, (2 * j0, 2 * j0 + 1, 2 * j1, 2 * j1 + 1), dy, dx)
        panel = jnp.concatenate([low[z], high[z]], axis=1)
        acc = acc + jnp.dot(panel, moved, preferred_element_type=jnp.float32)
    return acc


def squares_of(pairs):
    squares = jnp.zeros((ROWS, LANES), jnp.float32)
    for low, high, z, _ in pairs:
        for ref in (low, high):
            value = ref[z].astype(jnp.float32)
            squares = squares + value * value
    return squares


def pairs_of(refs, offsets):
    return [(*ref, z, dy) for ref, dy in zip(refs, offsets) for z in range(4)]


def halves(ref):
    return ref.at[0:4], ref.at[4:8]


def first_kernel(shift_ref, t_ref, pc, py1, py3, s_ref, n_ref):
    pairs = pairs_of((halves(pc), halves(py1), halves(py3)), (0, -1, 1))
    n_ref[...] = squares_of(pairs)

    def one_shift(s, carry):
        s_ref[s] = add_scores(shift_ref, t_ref, pairs, s)
        return carry

    lax.fori_loop(0, SHIFTS, one_shift, 0, unroll=True)


def last_kernel(shift_ref, t_ref, pw0, pw1, s_in, n_in, rot_ref, info_ref, e_ref, st_ref):
    gain = SCORE_GAIN / math.sqrt(PIX)
    pairs = pairs_of(((pw0, pw1),), (2,))
    norms = jnp.sum(n_in[...] + squares_of(pairs), axis=1, keepdims=True)
    rots = jnp.concatenate([rot_ref[0], rot_ref[1]], axis=1)
    angle = rots[0:1] * (2.0 * math.pi / ROT)
    info = info_ref[...]
    prior = info[:, 1:2] * jnp.cos(angle) + info[:, 2:3] * jnp.sin(angle)
    bias = info[:, 0:1] - 0.5 * gain * norms + PRIOR_WEIGHT * prior
    is_panel = lax.broadcasted_iota(jnp.int32, (ROWS, 1), 0) < USED
    bias = jnp.where(is_panel, bias, NEG)

    def one_shift(s, peak):
        scores = gain * (s_in[s] + add_scores(shift_ref, t_ref, pairs, s)) + bias
        e_ref[s] = scores
        return jnp.maximum(peak, jnp.max(scores, axis=0, keepdims=True))

    peak = lax.fori_loop(
        0, SHIFTS, one_shift, jnp.full((1, ROW_IMAGES), NEG, jnp.float32), unroll=True
    )

    def one_exp(s, total):
        value = jnp.exp(e_ref[s] - peak)
        e_ref[s] = value
        return total + jnp.sum(value, axis=0, keepdims=True)

    total = lax.fori_loop(
        0, SHIFTS, one_exp, jnp.zeros((1, ROW_IMAGES), jnp.float32), unroll=True
    )
    stats = jnp.concatenate(
        [
            peak[:, :LANES],
            peak[:, LANES:],
            total[:, :LANES],
            total[:, LANES:],
            jnp.zeros((4, LANES), jnp.float32),
        ],
        axis=0,
    )
    for k in range(8):
        st_ref[k] = stats


def far_kernel(shift_ref, e_ref, st_ref, all_ref, t_ref, out_ref, ev_ref, w_ref, tail_ref):
    x, core, _, _, _ = position()
    stats = [all_ref[k] for k in range(8)]
    peak = stats[0][0:2]
    for k in range(1, 8):
        peak = jnp.maximum(peak, stats[k][0:2])
    total = jnp.zeros((2, LANES), jnp.float32)
    for k in range(8):
        total = total + stats[k][2:4] * jnp.exp(stats[k][0:2] - peak)
    evidence = peak + jnp.log(total)
    slot = x * 2 + core
    mine = jnp.where(slot >= 4, evidence[1:2], evidence[0:1])
    groups = [mine[:, k * OWN : (k + 1) * OWN] for k in range(4)]
    at = jnp.bitwise_and(slot, 3)
    picked = groups[0]
    for k in range(1, 4):
        picked = jnp.where(at == k, groups[k], picked)
    ev_ref[...] = picked
    factor = jnp.exp(st_ref[0][0:2] - peak) / total
    factor = jnp.concatenate([factor[0:1], factor[1:2]], axis=1)

    for s in range(SHIFTS):
        weight = (e_ref[s] * factor).astype(jnp.bfloat16)
        w_ref[s * ROW_IMAGES : (s + 1) * ROW_IMAGES, :] = weight.T

    ones = jnp.ones((16, SHIFTS * ROW_IMAGES), jnp.bfloat16)
    totals = jnp.dot(ones, w_ref[...], preferred_element_type=jnp.float32)[0:1]
    totals = jnp.concatenate([totals, jnp.zeros((1, 2 * LANES - ROWS), jnp.float32)], axis=1)
    tail = split_tail(jnp.concatenate([totals[:, :LANES], totals[:, LANES:]], axis=0))
    tail_ref[...] = tail
    far = jnp.bitwise_and(position()[4] + 2, 3)
    for z in range(4):
        store_sums(out_ref, z, tile_sums(shift_ref, t_ref, w_ref, z, far), tail)


def tile_sums(shift_ref, t_ref, w_ref, z, y):
    low, high = 2 * (4 * z + y), 2 * (4 * z + y) + 2 * 16
    rows = (low, low + 1, high, high + 1)
    moved = jnp.concatenate(
        [shifted_pixels(t_ref, rows, shift_ref[0, s], shift_ref[1, s]) for s in range(SHIFTS)],
        axis=1,
    )
    return jnp.dot(moved, w_ref[...], preferred_element_type=jnp.float32)


def is_tail():
    row = lax.broadcasted_iota(jnp.int32, (16, LANES), 0)
    return row >= USED - (ROWS - 16)


def store_sums(out_ref, z, acc, tail):
    turned = acc.astype(jnp.bfloat16).T
    for k in range(2):
        part = turned[:, k * LANES : (k + 1) * LANES]
        out_ref[4 * k + z, 0 : ROWS - 16, :] = part[: ROWS - 16]
        out_ref[4 * k + z, ROWS - 16 : ROWS, :] = jnp.where(is_tail(), tail, part[ROWS - 16 :])


def near_kernel(shift_ref, w_ref, tail_ref, t_ref, up_ref, down_ref):
    y = position()[4]
    for step, out_ref in ((1, up_ref), (-1, down_ref)):
        for z in range(4):
            at = jnp.bitwise_and(y + step, 3)
            acc = tile_sums(shift_ref, t_ref, w_ref, z, at)
            store_sums(out_ref, z, acc, tail_ref[...])


def own_kernel(shift_ref, w_ref, t_ref, after_ref, out_ref):
    del after_ref
    y = position()[4]
    for z in range(4):
        turned = tile_sums(shift_ref, t_ref, w_ref, z, y).T
        for k in range(2):
            out_ref[4 * k + z] = turned[:, k * LANES : (k + 1) * LANES]


def split_tail(totals):
    pieces = []
    for _ in range(3):
        part = totals.astype(jnp.bfloat16).astype(jnp.float32)
        totals = totals - part
        pieces.append(part)
    lead = jnp.zeros((USED - (ROWS - 16), LANES), jnp.float32)
    rest = jnp.zeros((ROWS - USED - 6, LANES), jnp.float32)
    return jnp.concatenate([lead] + pieces + [rest], axis=0).astype(jnp.bfloat16)


def joined_tail(tail):
    at = USED - (ROWS - 16)
    return tail[at : at + 2] + tail[at + 2 : at + 4] + tail[at + 4 : at + 6]


def add_kernel(own_ref, tail_ref, far_ref, up_ref, down_ref, out_ref):
    others = (far_ref, up_ref, down_ref)
    totals = joined_tail(tail_ref[...].astype(jnp.float32))
    for ref in others:
        totals = totals + joined_tail(ref[0, ROWS - 16 : ROWS, :].astype(jnp.float32))
    tail = split_tail(totals)
    for k in range(8):
        acc = own_ref[k]
        for ref in others:
            acc = acc + ref[k].astype(jnp.float32)
        acc = acc.astype(jnp.bfloat16)
        out_ref[k, 0 : ROWS - 16, :] = acc[: ROWS - 16]
        out_ref[k, ROWS - 16 : ROWS, :] = jnp.where(is_tail(), tail, acc[ROWS - 16 :])


def finish_kernel(in_ref, out_ref, wt_ref):
    for half in range(2):
        acc = jnp.zeros((ROWS, LANES), jnp.float32)
        for k in range(4):
            acc = acc + in_ref[half * 4 + k].astype(jnp.float32)
        for r in range(HALF_ROT):
            out_ref[half * HALF_ROT + r] = acc[r * CLS : (r + 1) * CLS]
        wide = joined_tail(acc[ROWS - 16 :])
        totals = jnp.concatenate([wide[0:1], wide[1:2]], axis=1)
        for r in range(HALF_ROT):
            row = half * HALF_ROT + r
            wt_ref[row : row + 1, :] = totals[:, r * CLS : (r + 1) * CLS]


VMEM = pl.BlockSpec(memory_space=pltpu.VMEM)
SMEM = pl.BlockSpec(memory_space=pltpu.SMEM)
PARAMS = pltpu.CompilerParams(vmem_limit_bytes=40 * 1024 * 1024)


def cost(quarters, megabytes):
    flops = 1000 * quarters
    return pl.CostEstimate(flops=flops, bytes_accessed=1000 * megabytes, transcendentals=0)


def shards(particles, rot_prior, panels, log_prior, shift_table):
    spread, images, info = pl.pallas_call(
        prepare_kernel,
        out_shape=(
            jax.ShapeDtypeStruct((8, ROWS, LANES), jnp.bfloat16),
            jax.ShapeDtypeStruct((OWN, PIX + LANES), jnp.bfloat16),
            jax.ShapeDtypeStruct((ROWS, LANES), jnp.float32),
        ),
        in_specs=[pl.BlockSpec(memory_space=pltpu.HBM)] * 4,
        out_specs=(VMEM,) * 3,
        scratch_shapes=[
            pltpu.VMEM((ROT, CLS, LANES), jnp.bfloat16),
            pltpu.VMEM((OWN, PIX), jnp.float32),
            pltpu.VMEM((1, OWN), jnp.int32),
            pltpu.VMEM((1, CLS), jnp.float32),
            pltpu.VMEM((2, ROWS, LANES), jnp.float32),
            pltpu.SemaphoreType.DMA((4,)),
        ],
        compiler_params=pltpu.CompilerParams(vmem_limit_bytes=60 * 1024 * 1024),
        cost_estimate=cost(0, 1),
        name="prepare",
    )(
        jnp.transpose(panels, (1, 0, 2)),
        particles,
        rot_prior.reshape(1, OWN),
        log_prior.reshape(1, CLS),
    )
    a1 = move(images, x=1)
    a2 = move(images, x=-1)
    a3 = move(images, x=2)
    column = lax.all_to_all(spread, "img", 0, 0, axis_index_groups=XZ_GROUPS)
    y1 = move(column, y=1)
    y3 = move(column, y=-1)
    mine = jnp.concatenate([images, a1, a2, a3], axis=0)
    mine, y1, y3 = lax.optimization_barrier((mine, y1, y3))
    cc = move(mine, core=1)
    yw0 = move(y1[:4], y=1)
    yw1 = move(y3[4:], y=-1)

    turned, rots = pl.pallas_call(
        turn_kernel,
        out_shape=(
            jax.ShapeDtypeStruct((2, SIDE, SIDE + 2 * MARGIN, LANES), jnp.float32),
            jax.ShapeDtypeStruct((2, 8, LANES), jnp.float32),
        ),
        in_specs=[VMEM] * 2,
        out_specs=(VMEM, VMEM),
        scratch_shapes=[pltpu.VMEM((ROW_IMAGES, PIX + LANES), jnp.bfloat16)],
        compiler_params=PARAMS,
        cost_estimate=cost(0, 8),
        name="turn",
    )(mine, cc)

    shifts = shift_table.T
    score_shape = jax.ShapeDtypeStruct((SHIFTS, ROWS, ROW_IMAGES), jnp.float32)
    norm_shape = jax.ShapeDtypeStruct((ROWS, LANES), jnp.float32)
    scores, norms = pl.pallas_call(
        first_kernel,
        out_shape=(score_shape, norm_shape),
        in_specs=[SMEM] + [VMEM] * 4,
        out_specs=(VMEM, VMEM),
        compiler_params=PARAMS,
        cost_estimate=cost(3, 4),
        name="first",
    )(shifts, turned, column, y1, y3)

    scores, stats = pl.pallas_call(
        last_kernel,
        out_shape=(score_shape, jax.ShapeDtypeStruct((8, 8, LANES), jnp.float32)),
        in_specs=[SMEM] + [VMEM] * 7,
        out_specs=(VMEM, VMEM),
        input_output_aliases={4: 0},
        compiler_params=PARAMS,
        cost_estimate=cost(1, 8),
        name="last",
    )(shifts, turned, yw0, yw1, scores, norms, rots, info)
    all_stats = lax.all_to_all(stats, AXES, 0, 0, axis_index_groups=X_ROWS)
    block_shape = jax.ShapeDtypeStruct((8, ROWS, LANES), jnp.bfloat16)
    far, evidence, weights, tail = pl.pallas_call(
        far_kernel,
        out_shape=(
            block_shape,
            jax.ShapeDtypeStruct((1, OWN), jnp.float32),
            jax.ShapeDtypeStruct((SHIFTS * ROW_IMAGES, ROWS), jnp.bfloat16),
            jax.ShapeDtypeStruct((16, LANES), jnp.bfloat16),
        ),
        in_specs=[SMEM] + [VMEM] * 4,
        out_specs=(VMEM,) * 4,
        compiler_params=PARAMS,
        cost_estimate=cost(1, 4),
        name="far",
    )(shifts, scores, stats, all_stats, turned)
    from_far = move(far, y=2)
    up, down = pl.pallas_call(
        near_kernel,
        out_shape=(block_shape,) * 2,
        in_specs=[SMEM] + [VMEM] * 3,
        out_specs=(VMEM,) * 2,
        compiler_params=PARAMS,
        cost_estimate=cost(2, 4),
        name="near",
    )(shifts, weights, tail, turned)
    from_down = move(up, y=1)
    from_up = move(down, y=-1)
    own = pl.pallas_call(
        own_kernel,
        out_shape=jax.ShapeDtypeStruct((8, ROWS, LANES), jnp.float32),
        in_specs=[SMEM] + [VMEM] * 2 + [pl.BlockSpec(memory_space=pl.ANY)],
        out_specs=VMEM,
        compiler_params=PARAMS,
        cost_estimate=cost(1, 4),
        name="own",
    )(shifts, weights, turned, up)
    column_sums = pl.pallas_call(
        add_kernel,
        out_shape=block_shape,
        in_specs=[VMEM] * 5,
        out_specs=VMEM,
        compiler_params=PARAMS,
        cost_estimate=cost(0, 2),
        name="add",
    )(own, tail, from_far, from_down, from_up)
    shares = lax.all_to_all(column_sums, "img", 0, 0, axis_index_groups=XZ_GROUPS)
    sums, totals = pl.pallas_call(
        finish_kernel,
        out_shape=(
            jax.ShapeDtypeStruct((ROT, CLS, LANES), jnp.float32),
            jax.ShapeDtypeStruct((ROT, CLS), jnp.float32),
        ),
        in_specs=[VMEM],
        out_specs=(VMEM, VMEM),
        compiler_params=PARAMS,
        name="finish",
    )(shares)
    return jnp.transpose(sums, (1, 0, 2)), totals.T, evidence.reshape(OWN)


def solution(mesh):
    placed = (P(AXES, None), P(AXES), P("cls", None, "img"), P("cls"), P())
    return jax.shard_map(
        shards,
        mesh=mesh,
        in_specs=placed,
        out_specs=(P("cls", None, "img"), P("cls", None), P(AXES)),
        check_vma=False,
    )
```

```python
import math

import jax
import jax.numpy as jnp
from jax import lax
from jax.experimental import pallas as pl
from jax.experimental.pallas import tpu as pltpu
from jax.sharding import PartitionSpec as P

SCORE_GAIN = 2.5
PRIOR_WEIGHT = 1.0
AXES = ("cls", "img")
SIDE = 64
PIX = SIDE * SIDE
LANES = 128
BLOCKS = PIX // LANES
ROT = 12
HALF_ROT = ROT // 2
CLS = 25
USED = HALF_ROT * CLS
ROWS = 160
OWN = 32
ROW_IMAGES = 8 * OWN
SHIFTS = 11
MARGIN = 8
NEG = -1.0e30


def flat(x, core, z, y):
    x %= 4
    return ((x // 2) * 2 + core % 2) * 32 + (x % 2) * 16 + (z % 4) * 4 + y % 4


COORDS = [(x, c, z, y) for x in range(4) for c in range(2) for z in range(4) for y in range(4)]
XZ_GROUPS = [[x * 16 + z * 4 + y for x in range(2) for z in range(4)] for y in range(4)]
X_ROWS = [[flat(x, c, z, y) for x in range(4) for c in range(2)] for z in range(4) for y in range(4)]


def move(value, x=0, core=0, z=0, y=0):
    route = [(flat(*a), flat(a[0] + x, a[1] + core, a[2] + z, a[3] + y)) for a in COORDS]
    return lax.ppermute(value, AXES, route)


def position():
    cls, img = lax.axis_index("cls"), lax.axis_index("img")
    x_lo, z, y = img // 16, (img // 4) % 4, img % 4
    return (cls // 2) * 2 + x_lo, cls % 2, x_lo, z, y


def shifted_pixels(t_ref, rows, dy, dx):
    parts = []
    for row in rows:
        at = jnp.bitwise_and(row + dy, SIDE - 1)
        tiles = [t_ref[t, at, pl.ds(MARGIN + dx, SIDE), :] for t in range(2)]
        parts.append(jnp.concatenate(tiles, axis=1).astype(jnp.bfloat16))
    return jnp.concatenate(parts, axis=0)


def prepare_kernel(*refs):
    sources, (send_ref, out_ref, info_ref) = refs[:4], refs[4:7]
    targets, half_ref, sems = refs[7:11], refs[11], refs[12]
    p_ref, x_ref, rot_ref, log_ref = targets
    _, _, x_lo, _, _ = position()
    copies = [
        pltpu.make_async_copy(sources[k], targets[k], sems.at[k]) for k in range(4)
    ]
    for copy in copies:
        copy.start()
    for copy in copies:
        copy.wait()
    for r in range(ROT):
        half, at = r // HALF_ROT, (r % HALF_ROT) * CLS
        half_ref[half, at : at + CLS, :] = p_ref[r].astype(jnp.float32)
    for half in range(2):
        half_ref[half, USED:ROWS, :] = jnp.zeros((ROWS - USED, LANES), jnp.float32)
    for half in range(2):
        value = half_ref[half].astype(jnp.bfloat16)
        for k in range(4):
            send_ref[4 * half + k] = value
    out_ref[:, 0:PIX] = x_ref[...].astype(jnp.bfloat16)
    rots = rot_ref[...].astype(jnp.float32)
    rots = jnp.concatenate([rots] * (LANES // OWN), axis=1)
    out_ref[:, PIX : PIX + LANES] = jnp.broadcast_to(rots, (OWN, LANES)).astype(jnp.bfloat16)
    diagonal = lax.broadcasted_iota(jnp.int32, (CLS, CLS), 0) == lax.broadcasted_iota(
        jnp.int32, (CLS, CLS), 1
    )
    logs = jnp.sum(jnp.where(diagonal, log_ref[...], 0.0), axis=1, keepdims=True)
    sign = (1 - 2 * x_lo).astype(jnp.float32)
    lane = lax.broadcasted_iota(jnp.int32, (CLS, LANES), 1)
    for r in range(HALF_ROT):
        turn = 2.0 * math.pi * r / ROT
        rows = jnp.where(lane == 1, math.cos(turn) * sign, math.sin(turn) * sign)
        info_ref[r * CLS : (r + 1) * CLS, :] = jnp.where(lane == 0, logs, rows)
    info_ref[USED:ROWS, :] = jnp.full((ROWS - USED, LANES), NEG, jnp.float32)


def turn_kernel(own, own_other, mine, other, t_ref, rot_ref, x_ref):
    x, core, _, _, _ = position()

    def put(value, dx, dc):
        slot = jnp.bitwise_and(x + dx, 3) * 2 + jnp.bitwise_xor(core, dc)
        x_ref[pl.ds(pl.multiple_of(slot * OWN, OWN), OWN), :] = value

    put(own[...], 0, 0)
    put(own_other[...], 0, 1)
    for k, dx in enumerate((-1, 1, 2)):
        put(mine[k * OWN : (k + 1) * OWN], dx, 0)
        put(other[k * OWN : (k + 1) * OWN], dx, 1)

    def turn_blocks(step, carry):
        for k in range(4):
            block = 4 * step + k
            lanes = pl.ds(pl.multiple_of(block * LANES, LANES), LANES)
            for t in range(2):
                tile = x_ref[pl.ds(t * LANES, LANES), lanes].astype(jnp.float32).T
                for half in range(2):
                    line = tile[half * SIDE : (half + 1) * SIDE]
                    t_ref[t, 2 * block + half, pl.ds(MARGIN, SIDE), :] = line
                    t_ref[t, 2 * block + half, pl.ds(0, MARGIN), :] = line[SIDE - MARGIN :]
                    t_ref[t, 2 * block + half, pl.ds(MARGIN + SIDE, MARGIN), :] = line[:MARGIN]
        return carry

    lax.fori_loop(0, BLOCKS // 4, turn_blocks, 0)
    lane_group = lax.broadcasted_iota(jnp.int32, (8, LANES), 1) // OWN
    for t in range(2):
        rots = jnp.zeros((8, LANES), jnp.float32)
        for k in range(4):
            start = t * LANES + k * OWN
            mine = x_ref[start : start + 16, PIX : PIX + LANES].astype(jnp.float32)[0:8]
            rots = jnp.where(lane_group == k, mine, rots)
        rot_ref[t] = rots


def add_scores(shift_ref, t_ref, pairs, s):
    y = position()[4]
    dy, dx = shift_ref[0, s], shift_ref[1, s]
    acc = jnp.zeros((ROWS, ROW_IMAGES), jnp.float32)
    for low, high, z, dyy in pairs:
        j0 = z * 4 + jnp.bitwise_and(y + dyy, 3)
        j1 = j0 + 16
        moved = shifted_pixels(t_ref, (2 * j0, 2 * j0 + 1, 2 * j1, 2 * j1 + 1), dy, dx)
        panel = jnp.concatenate([low[z], high[z]], axis=1)
        acc = acc + jnp.dot(panel, moved, preferred_element_type=jnp.float32)
    return acc


def squares_of(pairs):
    squares = jnp.zeros((ROWS, LANES), jnp.float32)
    for low, high, z, _ in pairs:
        for ref in (low, high):
            value = ref[z].astype(jnp.float32)
            squares = squares + value * value
    return squares


def pairs_of(refs, offsets):
    return [(*ref, z, dy) for ref, dy in zip(refs, offsets) for z in range(4)]


def halves(ref):
    return ref.at[0:4], ref.at[4:8]


def first_kernel(shift_ref, t_ref, pc, py1, py3, s_ref, n_ref):
    pairs = pairs_of((halves(pc), halves(py1), halves(py3)), (0, -1, 1))
    n_ref[...] = squares_of(pairs)

    def one_shift(s, carry):
        s_ref[s] = add_scores(shift_ref, t_ref, pairs, s)
        return carry

    lax.fori_loop(0, SHIFTS, one_shift, 0, unroll=True)


def last_kernel(shift_ref, t_ref, pw0, pw1, s_in, n_in, rot_ref, info_ref, e_ref, st_ref):
    gain = SCORE_GAIN / math.sqrt(PIX)
    pairs = pairs_of(((pw0, pw1),), (2,))
    norms = jnp.sum(n_in[...] + squares_of(pairs), axis=1, keepdims=True)
    rots = jnp.concatenate([rot_ref[0], rot_ref[1]], axis=1)
    angle = rots[0:1] * (2.0 * math.pi / ROT)
    info = info_ref[...]
    prior = info[:, 1:2] * jnp.cos(angle) + info[:, 2:3] * jnp.sin(angle)
    bias = info[:, 0:1] - 0.5 * gain * norms + PRIOR_WEIGHT * prior
    is_panel = lax.broadcasted_iota(jnp.int32, (ROWS, 1), 0) < USED
    bias = jnp.where(is_panel, bias, NEG)

    def one_shift(s, peak):
        scores = gain * (s_in[s] + add_scores(shift_ref, t_ref, pairs, s)) + bias
        e_ref[s] = scores
        return jnp.maximum(peak, jnp.max(scores, axis=0, keepdims=True))

    peak = lax.fori_loop(
        0, SHIFTS, one_shift, jnp.full((1, ROW_IMAGES), NEG, jnp.float32), unroll=True
    )

    def one_exp(s, total):
        value = jnp.exp(e_ref[s] - peak)
        e_ref[s] = value
        return total + jnp.sum(value, axis=0, keepdims=True)

    total = lax.fori_loop(
        0, SHIFTS, one_exp, jnp.zeros((1, ROW_IMAGES), jnp.float32), unroll=True
    )
    stats = jnp.concatenate(
        [
            peak[:, :LANES],
            peak[:, LANES:],
            total[:, :LANES],
            total[:, LANES:],
            jnp.zeros((4, LANES), jnp.float32),
        ],
        axis=0,
    )
    for k in range(8):
        st_ref[k] = stats


def far_kernel(shift_ref, e_ref, st_ref, all_ref, t_ref, out_ref, ev_ref, w_ref, tail_ref):
    x, core, _, _, _ = position()
    stats = [all_ref[k] for k in range(8)]
    peak = stats[0][0:2]
    for k in range(1, 8):
        peak = jnp.maximum(peak, stats[k][0:2])
    total = jnp.zeros((2, LANES), jnp.float32)
    for k in range(8):
        total = total + stats[k][2:4] * jnp.exp(stats[k][0:2] - peak)
    evidence = peak + jnp.log(total)
    slot = x * 2 + core
    mine = jnp.where(slot >= 4, evidence[1:2], evidence[0:1])
    groups = [mine[:, k * OWN : (k + 1) * OWN] for k in range(4)]
    at = jnp.bitwise_and(slot, 3)
    picked = groups[0]
    for k in range(1, 4):
        picked = jnp.where(at == k, groups[k], picked)
    ev_ref[...] = picked
    factor = jnp.exp(st_ref[0][0:2] - peak) / total
    factor = jnp.concatenate([factor[0:1], factor[1:2]], axis=1)

    for s in range(SHIFTS):
        weight = (e_ref[s] * factor).astype(jnp.bfloat16)
        w_ref[s * ROW_IMAGES : (s + 1) * ROW_IMAGES, :] = weight.T

    ones = jnp.ones((16, SHIFTS * ROW_IMAGES), jnp.bfloat16)
    totals = jnp.dot(ones, w_ref[...], preferred_element_type=jnp.float32)[0:1]
    totals = jnp.concatenate([totals, jnp.zeros((1, 2 * LANES - ROWS), jnp.float32)], axis=1)
    tail = split_tail(jnp.concatenate([totals[:, :LANES], totals[:, LANES:]], axis=0))
    tail_ref[...] = tail
    far = jnp.bitwise_and(position()[4] + 2, 3)
    for z in range(0, 4, GROUP):
        store_sums(out_ref, z, tile_sums(shift_ref, t_ref, w_ref, z, far), tail)


GROUP = 4


def tile_sums(shift_ref, t_ref, w_ref, z, y):
    tiles = []
    for k in range(GROUP):
        low = 2 * (4 * (z + k) + y)
        rows = (low, low + 1, low + 2 * 16, low + 2 * 16 + 1)
        tiles.append(
            jnp.concatenate(
                [
                    shifted_pixels(t_ref, rows, shift_ref[0, s], shift_ref[1, s])
                    for s in range(SHIFTS)
                ],
                axis=1,
            )
        )
    moved = jnp.concatenate(tiles, axis=0)
    return jnp.dot(moved, w_ref[...], preferred_element_type=jnp.float32)


def is_tail():
    row = lax.broadcasted_iota(jnp.int32, (16, LANES), 0)
    return row >= USED - (ROWS - 16)


def store_sums(out_ref, z, acc, tail):
    turned = acc.astype(jnp.bfloat16).T
    for k in range(2 * GROUP):
        part = turned[:, k * LANES : (k + 1) * LANES]
        at = 4 * (k % 2) + z + k // 2
        out_ref[at, 0 : ROWS - 16, :] = part[: ROWS - 16]
        out_ref[at, ROWS - 16 : ROWS, :] = jnp.where(is_tail(), tail, part[ROWS - 16 :])


def near_kernel(shift_ref, w_ref, tail_ref, t_ref, up_ref, down_ref):
    y = position()[4]
    for step, out_ref in ((1, up_ref), (-1, down_ref)):
        for z in range(0, 4, GROUP):
            at = jnp.bitwise_and(y + step, 3)
            acc = tile_sums(shift_ref, t_ref, w_ref, z, at)
            store_sums(out_ref, z, acc, tail_ref[...])


def own_kernel(shift_ref, w_ref, t_ref, after_ref, out_ref):
    del after_ref
    y = position()[4]
    for z in range(0, 4, GROUP):
        turned = tile_sums(shift_ref, t_ref, w_ref, z, y).T
        for k in range(2 * GROUP):
            out_ref[4 * (k % 2) + z + k // 2] = turned[:, k * LANES : (k + 1) * LANES]


def split_tail(totals):
    pieces = []
    for _ in range(3):
        part = totals.astype(jnp.bfloat16).astype(jnp.float32)
        totals = totals - part
        pieces.append(part)
    lead = jnp.zeros((USED - (ROWS - 16), LANES), jnp.float32)
    rest = jnp.zeros((ROWS - USED - 6, LANES), jnp.float32)
    return jnp.concatenate([lead] + pieces + [rest], axis=0).astype(jnp.bfloat16)


def joined_tail(tail):
    at = USED - (ROWS - 16)
    return tail[at : at + 2] + tail[at + 2 : at + 4] + tail[at + 4 : at + 6]


def add_kernel(own_ref, tail_ref, far_ref, up_ref, down_ref, out_ref):
    others = (far_ref, up_ref, down_ref)
    totals = joined_tail(tail_ref[...].astype(jnp.float32))
    for ref in others:
        totals = totals + joined_tail(ref[0, ROWS - 16 : ROWS, :].astype(jnp.float32))
    tail = split_tail(totals)
    for k in range(8):
        acc = own_ref[k]
        for ref in others:
            acc = acc + ref[k].astype(jnp.float32)
        acc = acc.astype(jnp.bfloat16)
        out_ref[k, 0 : ROWS - 16, :] = acc[: ROWS - 16]
        out_ref[k, ROWS - 16 : ROWS, :] = jnp.where(is_tail(), tail, acc[ROWS - 16 :])


def finish_kernel(in_ref, out_ref, wt_ref):
    for half in range(2):
        acc = jnp.zeros((ROWS, LANES), jnp.float32)
        for k in range(4):
            acc = acc + in_ref[half * 4 + k].astype(jnp.float32)
        for r in range(HALF_ROT):
            out_ref[half * HALF_ROT + r] = acc[r * CLS : (r + 1) * CLS]
        wide = joined_tail(acc[ROWS - 16 :])
        totals = jnp.concatenate([wide[0:1], wide[1:2]], axis=1)
        for r in range(HALF_ROT):
            row = half * HALF_ROT + r
            wt_ref[row : row + 1, :] = totals[:, r * CLS : (r + 1) * CLS]


VMEM = pl.BlockSpec(memory_space=pltpu.VMEM)
SMEM = pl.BlockSpec(memory_space=pltpu.SMEM)
PARAMS = pltpu.CompilerParams(vmem_limit_bytes=40 * 1024 * 1024)


def cost(quarters, megabytes):
    flops = 1000 * quarters
    return pl.CostEstimate(flops=flops, bytes_accessed=1000 * megabytes, transcendentals=0)


def shards(particles, rot_prior, panels, log_prior, shift_table):
    spread, images, info = pl.pallas_call(
        prepare_kernel,
        out_shape=(
            jax.ShapeDtypeStruct((8, ROWS, LANES), jnp.bfloat16),
            jax.ShapeDtypeStruct((OWN, PIX + LANES), jnp.bfloat16),
            jax.ShapeDtypeStruct((ROWS, LANES), jnp.float32),
        ),
        in_specs=[pl.BlockSpec(memory_space=pltpu.HBM)] * 4,
        out_specs=(VMEM,) * 3,
        scratch_shapes=[
            pltpu.VMEM((ROT, CLS, LANES), jnp.bfloat16),
            pltpu.VMEM((OWN, PIX), jnp.float32),
            pltpu.VMEM((1, OWN), jnp.int32),
            pltpu.VMEM((1, CLS), jnp.float32),
            pltpu.VMEM((2, ROWS, LANES), jnp.float32),
            pltpu.SemaphoreType.DMA((4,)),
        ],
        compiler_params=pltpu.CompilerParams(vmem_limit_bytes=60 * 1024 * 1024),
        cost_estimate=cost(0, 1),
        name="prepare",
    )(
        jnp.transpose(panels, (1, 0, 2)),
        particles,
        rot_prior.reshape(1, OWN),
        log_prior.reshape(1, CLS),
    )
    c0 = move(images, core=1)
    a1 = move(images, x=1)
    a2 = move(images, x=-1)
    a3 = move(images, x=2)
    column = lax.all_to_all(spread, "img", 0, 0, axis_index_groups=XZ_GROUPS)
    column, c0 = lax.optimization_barrier((column, c0))
    y1 = move(column, y=1)
    y3 = move(column, y=-1)
    mine = jnp.concatenate([a1, a2, a3], axis=0)
    mine, y1, y3 = lax.optimization_barrier((mine, y1, y3))
    cc = move(mine, core=1)
    yw0 = move(y1[:4], y=1)
    yw1 = move(y3[4:], y=-1)

    turned, rots = pl.pallas_call(
        turn_kernel,
        out_shape=(
            jax.ShapeDtypeStruct((2, SIDE, SIDE + 2 * MARGIN, LANES), jnp.float32),
            jax.ShapeDtypeStruct((2, 8, LANES), jnp.float32),
        ),
        in_specs=[VMEM] * 4,
        out_specs=(VMEM, VMEM),
        scratch_shapes=[pltpu.VMEM((ROW_IMAGES, PIX + LANES), jnp.bfloat16)],
        compiler_params=PARAMS,
        cost_estimate=cost(0, 8),
        name="turn",
    )(images, c0, mine, cc)

    shifts = shift_table.T
    score_shape = jax.ShapeDtypeStruct((SHIFTS, ROWS, ROW_IMAGES), jnp.float32)
    norm_shape = jax.ShapeDtypeStruct((ROWS, LANES), jnp.float32)
    scores, norms = pl.pallas_call(
        first_kernel,
        out_shape=(score_shape, norm_shape),
        in_specs=[SMEM] + [VMEM] * 4,
        out_specs=(VMEM, VMEM),
        compiler_params=PARAMS,
        cost_estimate=cost(3, 4),
        name="first",
    )(shifts, turned, column, y1, y3)

    scores, stats = pl.pallas_call(
        last_kernel,
        out_shape=(score_shape, jax.ShapeDtypeStruct((8, 8, LANES), jnp.float32)),
        in_specs=[SMEM] + [VMEM] * 7,
        out_specs=(VMEM, VMEM),
        input_output_aliases={4: 0},
        compiler_params=PARAMS,
        cost_estimate=cost(1, 8),
        name="last",
    )(shifts, turned, yw0, yw1, scores, norms, rots, info)
    all_stats = lax.all_to_all(stats, AXES, 0, 0, axis_index_groups=X_ROWS)
    block_shape = jax.ShapeDtypeStruct((8, ROWS, LANES), jnp.bfloat16)
    far, evidence, weights, tail = pl.pallas_call(
        far_kernel,
        out_shape=(
            block_shape,
            jax.ShapeDtypeStruct((1, OWN), jnp.float32),
            jax.ShapeDtypeStruct((SHIFTS * ROW_IMAGES, ROWS), jnp.bfloat16),
            jax.ShapeDtypeStruct((16, LANES), jnp.bfloat16),
        ),
        in_specs=[SMEM] + [VMEM] * 4,
        out_specs=(VMEM,) * 4,
        compiler_params=PARAMS,
        cost_estimate=cost(1, 4),
        name="far",
    )(shifts, scores, stats, all_stats, turned)
    from_far = move(far, y=2)
    up, down = pl.pallas_call(
        near_kernel,
        out_shape=(block_shape,) * 2,
        in_specs=[SMEM] + [VMEM] * 3,
        out_specs=(VMEM,) * 2,
        compiler_params=PARAMS,
        cost_estimate=cost(2, 4),
        name="near",
    )(shifts, weights, tail, turned)
    from_down = move(up, y=1)
    from_up = move(down, y=-1)
    own = pl.pallas_call(
        own_kernel,
        out_shape=jax.ShapeDtypeStruct((8, ROWS, LANES), jnp.float32),
        in_specs=[SMEM] + [VMEM] * 2 + [pl.BlockSpec(memory_space=pl.ANY)],
        out_specs=VMEM,
        compiler_params=PARAMS,
        cost_estimate=cost(1, 4),
        name="own",
    )(shifts, weights, turned, up)
    column_sums = pl.pallas_call(
        add_kernel,
        out_shape=block_shape,
        in_specs=[VMEM] * 5,
        out_specs=VMEM,
        compiler_params=PARAMS,
        cost_estimate=cost(0, 2),
        name="add",
    )(own, tail, from_far, from_down, from_up)
    shares = lax.all_to_all(column_sums, "img", 0, 0, axis_index_groups=XZ_GROUPS)
    sums, totals = pl.pallas_call(
        finish_kernel,
        out_shape=(
            jax.ShapeDtypeStruct((ROT, CLS, LANES), jnp.float32),
            jax.ShapeDtypeStruct((ROT, CLS), jnp.float32),
        ),
        in_specs=[VMEM],
        out_specs=(VMEM, VMEM),
        compiler_params=PARAMS,
        name="finish",
    )(shares)
    return jnp.transpose(sums, (1, 0, 2)), totals.T, evidence.reshape(OWN)


def solution(mesh):
    placed = (P(AXES, None), P(AXES), P("cls", None, "img"), P("cls"), P())
    return jax.shard_map(
        shards,
        mesh=mesh,
        in_specs=placed,
        out_specs=(P("cls", None, "img"), P("cls", None), P(AXES)),
        check_vma=False,
    )
```

```python
import math

import jax
import jax.numpy as jnp
from jax import lax
from jax.experimental import pallas as pl
from jax.experimental.pallas import tpu as pltpu
from jax.sharding import PartitionSpec as P

SCORE_GAIN = 2.5
PRIOR_WEIGHT = 1.0
AXES = ("cls", "img")
SIDE = 64
PIX = SIDE * SIDE
LANES = 128
BLOCKS = PIX // LANES
ROT = 12
HALF_ROT = ROT // 2
CLS = 25
USED = HALF_ROT * CLS
ROWS = 160
OWN = 32
ROW_IMAGES = 8 * OWN
SHIFTS = 11
MARGIN = 8
NEG = -1.0e30


def flat(x, core, z, y):
    x %= 4
    return ((x // 2) * 2 + core % 2) * 32 + (x % 2) * 16 + (z % 4) * 4 + y % 4


COORDS = [(x, c, z, y) for x in range(4) for c in range(2) for z in range(4) for y in range(4)]
XZ_GROUPS = [[x * 16 + z * 4 + y for x in range(2) for z in range(4)] for y in range(4)]
X_ROWS = [[flat(x, c, z, y) for x in range(4) for c in range(2)] for z in range(4) for y in range(4)]


def move(value, x=0, core=0, z=0, y=0):
    route = [(flat(*a), flat(a[0] + x, a[1] + core, a[2] + z, a[3] + y)) for a in COORDS]
    return lax.ppermute(value, AXES, route)


def position():
    cls, img = lax.axis_index("cls"), lax.axis_index("img")
    x_lo, z, y = img // 16, (img // 4) % 4, img % 4
    return (cls // 2) * 2 + x_lo, cls % 2, x_lo, z, y


def shifted_pixels(t_ref, rows, dy, dx):
    parts = []
    for row in rows:
        at = jnp.bitwise_and(row + dy, SIDE - 1)
        tiles = [t_ref[t, at, pl.ds(MARGIN + dx, SIDE), :] for t in range(2)]
        parts.append(jnp.concatenate(tiles, axis=1).astype(jnp.bfloat16))
    return jnp.concatenate(parts, axis=0)


def prepare_kernel(*refs):
    sources, (send_out, image_out, info_out) = refs[:4], refs[4:7]
    targets, (half_ref, send_ref, out_ref, info_ref, sems, out_sems) = refs[7:11], refs[11:]
    p_ref, x_ref, rot_ref, log_ref = targets
    _, _, x_lo, _, _ = position()
    copies = [
        pltpu.make_async_copy(sources[k], targets[k], sems.at[k]) for k in range(4)
    ]
    for copy in copies:
        copy.start()
    copies[0].wait()
    for r in range(ROT):
        half, at = r // HALF_ROT, (r % HALF_ROT) * CLS
        half_ref[half, at : at + CLS, :] = p_ref[r].astype(jnp.float32)
    for half in range(2):
        half_ref[half, USED:ROWS, :] = jnp.zeros((ROWS - USED, LANES), jnp.float32)
    for half in range(2):
        value = half_ref[half].astype(jnp.bfloat16)
        for k in range(4):
            send_ref[4 * half + k] = value
    sent = [pltpu.make_async_copy(send_ref, send_out, out_sems.at[0])]
    sent[0].start()
    for copy in copies[1:]:
        copy.wait()
    out_ref[:, 0:PIX] = x_ref[...].astype(jnp.bfloat16)
    rots = rot_ref[...].astype(jnp.float32)
    rots = jnp.concatenate([rots] * (LANES // OWN), axis=1)
    out_ref[:, PIX : PIX + LANES] = jnp.broadcast_to(rots, (OWN, LANES)).astype(jnp.bfloat16)
    sent.append(pltpu.make_async_copy(out_ref, image_out, out_sems.at[1]))
    sent[1].start()
    diagonal = lax.broadcasted_iota(jnp.int32, (CLS, CLS), 0) == lax.broadcasted_iota(
        jnp.int32, (CLS, CLS), 1
    )
    logs = jnp.sum(jnp.where(diagonal, log_ref[...], 0.0), axis=1, keepdims=True)
    sign = (1 - 2 * x_lo).astype(jnp.float32)
    lane = lax.broadcasted_iota(jnp.int32, (CLS, LANES), 1)
    for r in range(HALF_ROT):
        turn = 2.0 * math.pi * r / ROT
        rows = jnp.where(lane == 1, math.cos(turn) * sign, math.sin(turn) * sign)
        info_ref[r * CLS : (r + 1) * CLS, :] = jnp.where(lane == 0, logs, rows)
    info_ref[USED:ROWS, :] = jnp.full((ROWS - USED, LANES), NEG, jnp.float32)
    sent.append(pltpu.make_async_copy(info_ref, info_out, out_sems.at[2]))
    sent[2].start()
    for copy in sent:
        copy.wait()


def turn_kernel(own, own_other, mine, other, t_ref, rot_ref, x_ref):
    x, core, _, _, _ = position()

    def put(value, dx, dc):
        slot = jnp.bitwise_and(x + dx, 3) * 2 + jnp.bitwise_xor(core, dc)
        x_ref[pl.ds(pl.multiple_of(slot * OWN, OWN), OWN), :] = value

    put(own[...], 0, 0)
    put(own_other[...], 0, 1)
    for k, dx in enumerate((-1, 1, 2)):
        put(mine[k * OWN : (k + 1) * OWN], dx, 0)
        put(other[k * OWN : (k + 1) * OWN], dx, 1)

    def turn_blocks(step, carry):
        for k in range(4):
            block = 4 * step + k
            lanes = pl.ds(pl.multiple_of(block * LANES, LANES), LANES)
            for t in range(2):
                tile = x_ref[pl.ds(t * LANES, LANES), lanes].astype(jnp.float32).T
                for half in range(2):
                    line = tile[half * SIDE : (half + 1) * SIDE]
                    t_ref[t, 2 * block + half, pl.ds(MARGIN, SIDE), :] = line
                    t_ref[t, 2 * block + half, pl.ds(0, MARGIN), :] = line[SIDE - MARGIN :]
                    t_ref[t, 2 * block + half, pl.ds(MARGIN + SIDE, MARGIN), :] = line[:MARGIN]
        return carry

    lax.fori_loop(0, BLOCKS // 4, turn_blocks, 0)
    lane_group = lax.broadcasted_iota(jnp.int32, (8, LANES), 1) // OWN
    for t in range(2):
        rots = jnp.zeros((8, LANES), jnp.float32)
        for k in range(4):
            start = t * LANES + k * OWN
            mine = x_ref[start : start + 16, PIX : PIX + LANES].astype(jnp.float32)[0:8]
            rots = jnp.where(lane_group == k, mine, rots)
        rot_ref[t] = rots


def add_scores(shift_ref, t_ref, pairs, s):
    y = position()[4]
    dy, dx = shift_ref[0, s], shift_ref[1, s]
    acc = jnp.zeros((ROWS, ROW_IMAGES), jnp.float32)
    for low, high, z, dyy in pairs:
        j0 = z * 4 + jnp.bitwise_and(y + dyy, 3)
        j1 = j0 + 16
        moved = shifted_pixels(t_ref, (2 * j0, 2 * j0 + 1, 2 * j1, 2 * j1 + 1), dy, dx)
        panel = jnp.concatenate([low[z], high[z]], axis=1)
        acc = acc + jnp.dot(panel, moved, preferred_element_type=jnp.float32)
    return acc


def squares_of(pairs):
    squares = jnp.zeros((ROWS, LANES), jnp.float32)
    for low, high, z, _ in pairs:
        for ref in (low, high):
            value = ref[z].astype(jnp.float32)
            squares = squares + value * value
    return squares


def pairs_of(refs, offsets):
    return [(*ref, z, dy) for ref, dy in zip(refs, offsets) for z in range(4)]


def halves(ref):
    return ref.at[0:4], ref.at[4:8]


def first_kernel(shift_ref, t_ref, pc, py1, py3, s_ref, n_ref):
    pairs = pairs_of((halves(pc), halves(py1), halves(py3)), (0, -1, 1))
    n_ref[...] = squares_of(pairs)

    def one_shift(s, carry):
        s_ref[s] = add_scores(shift_ref, t_ref, pairs, s)
        return carry

    lax.fori_loop(0, SHIFTS, one_shift, 0, unroll=True)


def last_kernel(shift_ref, t_ref, pw0, pw1, s_in, n_in, rot_ref, info_ref, e_ref, st_ref, m_ref):
    gain = SCORE_GAIN / math.sqrt(PIX)
    pairs = pairs_of(((pw0, pw1),), (2,))
    norms = jnp.sum(n_in[...] + squares_of(pairs), axis=1, keepdims=True)
    rots = jnp.concatenate([rot_ref[0], rot_ref[1]], axis=1)
    angle = rots[0:1] * (2.0 * math.pi / ROT)
    info = info_ref[...]
    prior = info[:, 1:2] * jnp.cos(angle) + info[:, 2:3] * jnp.sin(angle)
    bias = info[:, 0:1] - 0.5 * gain * norms + PRIOR_WEIGHT * prior
    is_panel = lax.broadcasted_iota(jnp.int32, (ROWS, 1), 0) < USED
    bias = jnp.where(is_panel, bias, NEG)

    peaks, sums = [], []
    for s in range(SHIFTS):
        scores = gain * (s_in[s] + add_scores(shift_ref, t_ref, pairs, s)) + bias
        peaks.append(jnp.max(scores, axis=0, keepdims=True))
        value = jnp.exp(scores - peaks[s])
        e_ref[s] = value
        sums.append(jnp.sum(value, axis=0, keepdims=True))
        m_ref[s : s + 1, :] = peaks[s]
    m_ref[SHIFTS:16, :] = jnp.zeros((16 - SHIFTS, ROW_IMAGES), jnp.float32)
    peak = peaks[0]
    for s in range(1, SHIFTS):
        peak = jnp.maximum(peak, peaks[s])
    total = jnp.zeros((1, ROW_IMAGES), jnp.float32)
    for s in range(SHIFTS):
        total = total + sums[s] * jnp.exp(peaks[s] - peak)
    stats = jnp.concatenate(
        [
            peak[:, :LANES],
            peak[:, LANES:],
            total[:, :LANES],
            total[:, LANES:],
            jnp.zeros((4, LANES), jnp.float32),
        ],
        axis=0,
    )
    for k in range(8):
        st_ref[k] = stats


def far_kernel(shift_ref, e_ref, m_ref, all_ref, t_ref, out_ref, ev_ref, w_ref, tail_ref):
    x, core, _, _, _ = position()
    stats = [all_ref[k] for k in range(8)]
    peak = stats[0][0:2]
    for k in range(1, 8):
        peak = jnp.maximum(peak, stats[k][0:2])
    total = jnp.zeros((2, LANES), jnp.float32)
    for k in range(8):
        total = total + stats[k][2:4] * jnp.exp(stats[k][0:2] - peak)
    evidence = peak + jnp.log(total)
    slot = x * 2 + core
    mine = jnp.where(slot >= 4, evidence[1:2], evidence[0:1])
    groups = [mine[:, k * OWN : (k + 1) * OWN] for k in range(4)]
    at = jnp.bitwise_and(slot, 3)
    picked = groups[0]
    for k in range(1, 4):
        picked = jnp.where(at == k, groups[k], picked)
    ev_ref[...] = picked
    peak = jnp.concatenate([peak[0:1], peak[1:2]], axis=1)
    total = jnp.concatenate([total[0:1], total[1:2]], axis=1)

    for s in range(SHIFTS):
        factor = jnp.exp(m_ref[s : s + 1, :] - peak) / total
        weight = (e_ref[s] * factor).astype(jnp.bfloat16)
        w_ref[s * ROW_IMAGES : (s + 1) * ROW_IMAGES, :] = weight.T

    ones = jnp.ones((16, SHIFTS * ROW_IMAGES), jnp.bfloat16)
    totals = jnp.dot(ones, w_ref[...], preferred_element_type=jnp.float32)[0:1]
    totals = jnp.concatenate([totals, jnp.zeros((1, 2 * LANES - ROWS), jnp.float32)], axis=1)
    tail = split_tail(jnp.concatenate([totals[:, :LANES], totals[:, LANES:]], axis=0))
    tail_ref[...] = tail
    far = jnp.bitwise_and(position()[4] + 2, 3)
    for z in range(0, 4, GROUP):
        store_sums(out_ref, z, tile_sums(shift_ref, t_ref, w_ref, z, far), tail)


GROUP = 4


def tile_sums(shift_ref, t_ref, w_ref, z, *ys):
    tiles = []
    for y, k in [(y, k) for y in ys for k in range(GROUP)]:
        low = 2 * (4 * (z + k) + y)
        rows = (low, low + 1, low + 2 * 16, low + 2 * 16 + 1)
        tiles.append(
            jnp.concatenate(
                [
                    shifted_pixels(t_ref, rows, shift_ref[0, s], shift_ref[1, s])
                    for s in range(SHIFTS)
                ],
                axis=1,
            )
        )
    moved = jnp.concatenate(tiles, axis=0)
    return jnp.dot(moved, w_ref[...], preferred_element_type=jnp.float32)


def is_tail():
    row = lax.broadcasted_iota(jnp.int32, (16, LANES), 0)
    return row >= USED - (ROWS - 16)


def store_sums(out_ref, z, acc, tail):
    turned = acc.astype(jnp.bfloat16).T
    for k in range(2 * GROUP):
        part = turned[:, k * LANES : (k + 1) * LANES]
        at = 4 * (k % 2) + z + k // 2
        out_ref[at, 0 : ROWS - 16, :] = part[: ROWS - 16]
        out_ref[at, ROWS - 16 : ROWS, :] = jnp.where(is_tail(), tail, part[ROWS - 16 :])


def near_kernel(shift_ref, w_ref, tail_ref, t_ref, up_ref, down_ref):
    y = position()[4]
    ahead, behind = jnp.bitwise_and(y + 1, 3), jnp.bitwise_and(y - 1, 3)
    size = 2 * LANES * GROUP
    for z in range(0, 4, GROUP):
        acc = tile_sums(shift_ref, t_ref, w_ref, z, ahead, behind)
        store_sums(up_ref, z, acc[:size], tail_ref[...])
        store_sums(down_ref, z, acc[size:], tail_ref[...])


def own_kernel(shift_ref, w_ref, t_ref, after_ref, out_ref):
    del after_ref
    y = position()[4]
    for z in range(0, 4, GROUP):
        turned = tile_sums(shift_ref, t_ref, w_ref, z, y).T
        for k in range(2 * GROUP):
            out_ref[4 * (k % 2) + z + k // 2] = turned[:, k * LANES : (k + 1) * LANES]


def split_tail(totals):
    pieces = []
    for _ in range(3):
        part = totals.astype(jnp.bfloat16).astype(jnp.float32)
        totals = totals - part
        pieces.append(part)
    lead = jnp.zeros((USED - (ROWS - 16), LANES), jnp.float32)
    rest = jnp.zeros((ROWS - USED - 6, LANES), jnp.float32)
    return jnp.concatenate([lead] + pieces + [rest], axis=0).astype(jnp.bfloat16)


def joined_tail(tail):
    at = USED - (ROWS - 16)
    return tail[at : at + 2] + tail[at + 2 : at + 4] + tail[at + 4 : at + 6]


def add_kernel(own_ref, tail_ref, far_ref, up_ref, down_ref, out_ref):
    others = (far_ref, up_ref, down_ref)
    totals = joined_tail(tail_ref[...].astype(jnp.float32))
    for ref in others:
        totals = totals + joined_tail(ref[0, ROWS - 16 : ROWS, :].astype(jnp.float32))
    tail = split_tail(totals)
    for k in range(8):
        acc = own_ref[k]
        for ref in others:
            acc = acc + ref[k].astype(jnp.float32)
        acc = acc.astype(jnp.bfloat16)
        out_ref[k, 0 : ROWS - 16, :] = acc[: ROWS - 16]
        out_ref[k, ROWS - 16 : ROWS, :] = jnp.where(is_tail(), tail, acc[ROWS - 16 :])


def finish_kernel(in_ref, out_ref, wt_ref):
    for half in range(2):
        acc = jnp.zeros((ROWS, LANES), jnp.float32)
        for k in range(4):
            acc = acc + in_ref[half * 4 + k].astype(jnp.float32)
        for r in range(HALF_ROT):
            out_ref[half * HALF_ROT + r] = acc[r * CLS : (r + 1) * CLS]
        wide = joined_tail(acc[ROWS - 16 :])
        totals = jnp.concatenate([wide[0:1], wide[1:2]], axis=1)
        for r in range(HALF_ROT):
            row = half * HALF_ROT + r
            wt_ref[row : row + 1, :] = totals[:, r * CLS : (r + 1) * CLS]


VMEM = pl.BlockSpec(memory_space=pltpu.VMEM)
SMEM = pl.BlockSpec(memory_space=pltpu.SMEM)
PARAMS = pltpu.CompilerParams(vmem_limit_bytes=40 * 1024 * 1024)


def cost(quarters, megabytes):
    flops = 1000 * quarters
    return pl.CostEstimate(flops=flops, bytes_accessed=1000 * megabytes, transcendentals=0)


def shards(particles, rot_prior, panels, log_prior, shift_table):
    spread, images, info = pl.pallas_call(
        prepare_kernel,
        out_shape=(
            jax.ShapeDtypeStruct((8, ROWS, LANES), jnp.bfloat16),
            jax.ShapeDtypeStruct((OWN, PIX + LANES), jnp.bfloat16),
            jax.ShapeDtypeStruct((ROWS, LANES), jnp.float32),
        ),
        in_specs=[pl.BlockSpec(memory_space=pltpu.HBM)] * 4,
        out_specs=(pl.BlockSpec(memory_space=pltpu.HBM),) * 3,
        scratch_shapes=[
            pltpu.VMEM((ROT, CLS, LANES), jnp.bfloat16),
            pltpu.VMEM((OWN, PIX), jnp.float32),
            pltpu.VMEM((1, OWN), jnp.int32),
            pltpu.VMEM((1, CLS), jnp.float32),
            pltpu.VMEM((2, ROWS, LANES), jnp.float32),
            pltpu.VMEM((8, ROWS, LANES), jnp.bfloat16),
            pltpu.VMEM((OWN, PIX + LANES), jnp.bfloat16),
            pltpu.VMEM((ROWS, LANES), jnp.float32),
            pltpu.SemaphoreType.DMA((4,)),
            pltpu.SemaphoreType.DMA((3,)),
        ],
        compiler_params=pltpu.CompilerParams(vmem_limit_bytes=60 * 1024 * 1024),
        cost_estimate=cost(0, 1),
        name="prepare",
    )(
        jnp.transpose(panels, (1, 0, 2)),
        particles,
        rot_prior.reshape(1, OWN),
        log_prior.reshape(1, CLS),
    )
    c0 = move(images, core=1)
    a1 = move(images, x=1)
    a2 = move(images, x=-1)
    a3 = move(images, x=2)
    column = lax.all_to_all(spread, "img", 0, 0, axis_index_groups=XZ_GROUPS)
    column, c0 = lax.optimization_barrier((column, c0))
    y1 = move(column, y=1)
    y3 = move(column, y=-1)
    mine = jnp.concatenate([a1, a2, a3], axis=0)
    mine, y1, y3 = lax.optimization_barrier((mine, y1, y3))
    cc = move(mine, core=1)
    yw0 = move(y1[:4], y=1)
    yw1 = move(y3[4:], y=-1)

    turned, rots = pl.pallas_call(
        turn_kernel,
        out_shape=(
            jax.ShapeDtypeStruct((2, SIDE, SIDE + 2 * MARGIN, LANES), jnp.float32),
            jax.ShapeDtypeStruct((2, 8, LANES), jnp.float32),
        ),
        in_specs=[VMEM] * 4,
        out_specs=(VMEM, VMEM),
        scratch_shapes=[pltpu.VMEM((ROW_IMAGES, PIX + LANES), jnp.bfloat16)],
        compiler_params=PARAMS,
        cost_estimate=cost(0, 8),
        name="turn",
    )(images, c0, mine, cc)

    shifts = shift_table.T
    score_shape = jax.ShapeDtypeStruct((SHIFTS, ROWS, ROW_IMAGES), jnp.float32)
    norm_shape = jax.ShapeDtypeStruct((ROWS, LANES), jnp.float32)
    scores, norms = pl.pallas_call(
        first_kernel,
        out_shape=(score_shape, norm_shape),
        in_specs=[SMEM] + [VMEM] * 4,
        out_specs=(VMEM, VMEM),
        compiler_params=PARAMS,
        cost_estimate=cost(3, 4),
        name="first",
    )(shifts, turned, column, y1, y3)

    scores, stats, peaks = pl.pallas_call(
        last_kernel,
        out_shape=(
            score_shape,
            jax.ShapeDtypeStruct((8, 8, LANES), jnp.float32),
            jax.ShapeDtypeStruct((16, ROW_IMAGES), jnp.float32),
        ),
        in_specs=[SMEM] + [VMEM] * 7,
        out_specs=(VMEM,) * 3,
        input_output_aliases={4: 0},
        compiler_params=PARAMS,
        cost_estimate=cost(1, 8),
        name="last",
    )(shifts, turned, yw0, yw1, scores, norms, rots, info)
    all_stats = lax.all_to_all(stats, AXES, 0, 0, axis_index_groups=X_ROWS)
    block_shape = jax.ShapeDtypeStruct((8, ROWS, LANES), jnp.bfloat16)
    far, evidence, weights, tail = pl.pallas_call(
        far_kernel,
        out_shape=(
            block_shape,
            jax.ShapeDtypeStruct((1, OWN), jnp.float32),
            jax.ShapeDtypeStruct((SHIFTS * ROW_IMAGES, ROWS), jnp.bfloat16),
            jax.ShapeDtypeStruct((16, LANES), jnp.bfloat16),
        ),
        in_specs=[SMEM] + [VMEM] * 4,
        out_specs=(VMEM,) * 4,
        compiler_params=PARAMS,
        cost_estimate=cost(1, 4),
        name="far",
    )(shifts, scores, peaks, all_stats, turned)
    from_far = move(far, y=2)
    up, down = pl.pallas_call(
        near_kernel,
        out_shape=(block_shape,) * 2,
        in_specs=[SMEM] + [VMEM] * 3,
        out_specs=(VMEM,) * 2,
        compiler_params=PARAMS,
        cost_estimate=cost(2, 4),
        name="near",
    )(shifts, weights, tail, turned)
    from_down = move(up, y=1)
    from_up = move(down, y=-1)
    own = pl.pallas_call(
        own_kernel,
        out_shape=jax.ShapeDtypeStruct((8, ROWS, LANES), jnp.float32),
        in_specs=[SMEM] + [VMEM] * 2 + [pl.BlockSpec(memory_space=pl.ANY)],
        out_specs=VMEM,
        compiler_params=PARAMS,
        cost_estimate=cost(1, 4),
        name="own",
    )(shifts, weights, turned, up)
    column_sums = pl.pallas_call(
        add_kernel,
        out_shape=block_shape,
        in_specs=[VMEM] * 5,
        out_specs=VMEM,
        compiler_params=PARAMS,
        cost_estimate=cost(0, 2),
        name="add",
    )(own, tail, from_far, from_down, from_up)
    shares = lax.all_to_all(column_sums, "img", 0, 0, axis_index_groups=XZ_GROUPS)
    sums, totals = pl.pallas_call(
        finish_kernel,
        out_shape=(
            jax.ShapeDtypeStruct((ROT, CLS, LANES), jnp.float32),
            jax.ShapeDtypeStruct((ROT, CLS), jnp.float32),
        ),
        in_specs=[VMEM],
        out_specs=(VMEM, VMEM),
        compiler_params=PARAMS,
        name="finish",
    )(shares)
    return jnp.transpose(sums, (1, 0, 2)), totals.T, evidence.reshape(OWN)


def solution(mesh):
    placed = (P(AXES, None), P(AXES), P("cls", None, "img"), P("cls"), P())
    return jax.shard_map(
        shards,
        mesh=mesh,
        in_specs=placed,
        out_specs=(P("cls", None, "img"), P("cls", None), P(AXES)),
        check_vma=False,
    )
```

```python
import math

import jax
import jax.numpy as jnp
from jax import lax
from jax.experimental import pallas as pl
from jax.experimental.pallas import tpu as pltpu
from jax.sharding import PartitionSpec as P

SCORE_GAIN = 2.5
PRIOR_WEIGHT = 1.0
AXES = ("cls", "img")
SIDE = 64
PIX = SIDE * SIDE
LANES = 128
BLOCKS = PIX // LANES
ROT = 12
HALF_ROT = ROT // 2
CLS = 25
USED = HALF_ROT * CLS
ROWS = 160
OWN = 32
ROW_IMAGES = 8 * OWN
SHIFTS = 11
MARGIN = 8
NEG = -1.0e30


def flat(x, core, z, y):
    x %= 4
    return ((x // 2) * 2 + core % 2) * 32 + (x % 2) * 16 + (z % 4) * 4 + y % 4


COORDS = [(x, c, z, y) for x in range(4) for c in range(2) for z in range(4) for y in range(4)]
XZ_GROUPS = [[x * 16 + z * 4 + y for x in range(2) for z in range(4)] for y in range(4)]
X_ROWS = [[flat(x, c, z, y) for x in range(4) for c in range(2)] for z in range(4) for y in range(4)]


def move(value, x=0, core=0, z=0, y=0):
    route = [(flat(*a), flat(a[0] + x, a[1] + core, a[2] + z, a[3] + y)) for a in COORDS]
    return lax.ppermute(value, AXES, route)


def position():
    cls, img = lax.axis_index("cls"), lax.axis_index("img")
    x_lo, z, y = img // 16, (img // 4) % 4, img % 4
    return (cls // 2) * 2 + x_lo, cls % 2, x_lo, z, y


def shifted_pixels(t_ref, rows, dy, dx):
    parts = []
    for row in rows:
        at = jnp.bitwise_and(row + dy, SIDE - 1)
        tiles = [t_ref[t, at, pl.ds(MARGIN + dx, SIDE), :] for t in range(2)]
        parts.append(jnp.concatenate(tiles, axis=1).astype(jnp.bfloat16))
    return jnp.concatenate(parts, axis=0)


def prepare_kernel(*refs):
    sources, (send_out, image_out, info_out) = refs[:4], refs[4:7]
    targets, (half_ref, send_ref, out_ref, info_ref, sems, out_sems) = refs[7:11], refs[11:]
    p_ref, x_ref, rot_ref, log_ref = targets
    _, _, x_lo, _, _ = position()
    copies = [
        pltpu.make_async_copy(sources[k], targets[k], sems.at[k]) for k in range(4)
    ]
    for copy in copies:
        copy.start()
    copies[0].wait()
    for r in range(ROT):
        half, at = r // HALF_ROT, (r % HALF_ROT) * CLS
        half_ref[half, at : at + CLS, :] = p_ref[r].astype(jnp.float32)
    for half in range(2):
        half_ref[half, USED:ROWS, :] = jnp.zeros((ROWS - USED, LANES), jnp.float32)
    for half in range(2):
        value = half_ref[half].astype(jnp.bfloat16)
        for k in range(4):
            send_ref[4 * half + k] = value
    sent = [pltpu.make_async_copy(send_ref, send_out, out_sems.at[0])]
    sent[0].start()
    for copy in copies[1:]:
        copy.wait()
    out_ref[:, 0:PIX] = x_ref[...].astype(jnp.bfloat16)
    rots = rot_ref[...].astype(jnp.float32)
    rots = jnp.concatenate([rots] * (LANES // OWN), axis=1)
    out_ref[:, PIX : PIX + LANES] = jnp.broadcast_to(rots, (OWN, LANES)).astype(jnp.bfloat16)
    sent.append(pltpu.make_async_copy(out_ref, image_out, out_sems.at[1]))
    sent[1].start()
    diagonal = lax.broadcasted_iota(jnp.int32, (CLS, CLS), 0) == lax.broadcasted_iota(
        jnp.int32, (CLS, CLS), 1
    )
    logs = jnp.sum(jnp.where(diagonal, log_ref[...], 0.0), axis=1, keepdims=True)
    sign = (1 - 2 * x_lo).astype(jnp.float32)
    lane = lax.broadcasted_iota(jnp.int32, (CLS, LANES), 1)
    for r in range(HALF_ROT):
        turn = 2.0 * math.pi * r / ROT
        rows = jnp.where(lane == 1, math.cos(turn) * sign, math.sin(turn) * sign)
        info_ref[r * CLS : (r + 1) * CLS, :] = jnp.where(lane == 0, logs, rows)
    info_ref[USED:ROWS, :] = jnp.full((ROWS - USED, LANES), NEG, jnp.float32)
    sent.append(pltpu.make_async_copy(info_ref, info_out, out_sems.at[2]))
    sent[2].start()
    for copy in sent:
        copy.wait()


def turn_kernel(own, own_other, mine, other, t_ref, rot_ref, x_ref):
    x, core, _, _, _ = position()

    def put(value, dx, dc):
        slot = jnp.bitwise_and(x + dx, 3) * 2 + jnp.bitwise_xor(core, dc)
        x_ref[pl.ds(pl.multiple_of(slot * OWN, OWN), OWN), :] = value

    put(own[...], 0, 0)
    put(own_other[...], 0, 1)
    for k, dx in enumerate((-1, 1, 2)):
        put(mine[k * OWN : (k + 1) * OWN], dx, 0)
        put(other[k * OWN : (k + 1) * OWN], dx, 1)

    def turn_blocks(step, carry):
        for k in range(4):
            block = 4 * step + k
            lanes = pl.ds(pl.multiple_of(block * LANES, LANES), LANES)
            for t in range(2):
                tile = x_ref[pl.ds(t * LANES, LANES), lanes].astype(jnp.float32).T
                for half in range(2):
                    line = tile[half * SIDE : (half + 1) * SIDE]
                    t_ref[t, 2 * block + half, pl.ds(MARGIN, SIDE), :] = line
                    t_ref[t, 2 * block + half, pl.ds(0, MARGIN), :] = line[SIDE - MARGIN :]
                    t_ref[t, 2 * block + half, pl.ds(MARGIN + SIDE, MARGIN), :] = line[:MARGIN]
        return carry

    lax.fori_loop(0, BLOCKS // 4, turn_blocks, 0)
    lane_group = lax.broadcasted_iota(jnp.int32, (8, LANES), 1) // OWN
    for t in range(2):
        rots = jnp.zeros((8, LANES), jnp.float32)
        for k in range(4):
            start = t * LANES + k * OWN
            mine = x_ref[start : start + 16, PIX : PIX + LANES].astype(jnp.float32)[0:8]
            rots = jnp.where(lane_group == k, mine, rots)
        rot_ref[t] = rots


def add_scores(shift_ref, t_ref, pairs, s):
    y = position()[4]
    dy, dx = shift_ref[0, s], shift_ref[1, s]
    acc = jnp.zeros((ROWS, ROW_IMAGES), jnp.float32)
    for low, high, z, dyy in pairs:
        j0 = z * 4 + jnp.bitwise_and(y + dyy, 3)
        j1 = j0 + 16
        moved = shifted_pixels(t_ref, (2 * j0, 2 * j0 + 1, 2 * j1, 2 * j1 + 1), dy, dx)
        panel = jnp.concatenate([low[z], high[z]], axis=1)
        acc = acc + jnp.dot(panel, moved, preferred_element_type=jnp.float32)
    return acc


def squares_of(pairs):
    squares = jnp.zeros((ROWS, LANES), jnp.float32)
    for low, high, z, _ in pairs:
        for ref in (low, high):
            value = ref[z].astype(jnp.float32)
            squares = squares + value * value
    return squares


def pairs_of(refs, offsets):
    return [(*ref, z, dy) for ref, dy in zip(refs, offsets) for z in range(4)]


def halves(ref):
    return ref.at[0:4], ref.at[4:8]


def first_kernel(shift_ref, t_ref, pc, py1, py3, s_ref, n_ref):
    pairs = pairs_of((halves(pc), halves(py1), halves(py3)), (0, -1, 1))
    n_ref[...] = squares_of(pairs)

    def one_shift(s, carry):
        s_ref[s] = add_scores(shift_ref, t_ref, pairs, s)
        return carry

    lax.fori_loop(0, SHIFTS, one_shift, 0, unroll=True)


def last_kernel(shift_ref, t_ref, pw0, pw1, s_in, n_in, rot_ref, info_ref, e_ref, st_ref, m_ref):
    gain = SCORE_GAIN / math.sqrt(PIX)
    pairs = pairs_of(((pw0, pw1),), (2,))
    norms = jnp.sum(n_in[...] + squares_of(pairs), axis=1, keepdims=True)
    rots = jnp.concatenate([rot_ref[0], rot_ref[1]], axis=1)
    angle = rots[0:1] * (2.0 * math.pi / ROT)
    info = info_ref[...]
    prior = info[:, 1:2] * jnp.cos(angle) + info[:, 2:3] * jnp.sin(angle)
    bias = info[:, 0:1] - 0.5 * gain * norms + PRIOR_WEIGHT * prior
    is_panel = lax.broadcasted_iota(jnp.int32, (ROWS, 1), 0) < USED
    bias = jnp.where(is_panel, bias, NEG)

    peaks, sums = [], []
    for s in range(SHIFTS):
        scores = gain * (s_in[s] + add_scores(shift_ref, t_ref, pairs, s)) + bias
        peaks.append(jnp.max(scores, axis=0, keepdims=True))
        value = jnp.exp(scores - peaks[s])
        e_ref[s] = value
        sums.append(jnp.sum(value, axis=0, keepdims=True))
        m_ref[s : s + 1, :] = peaks[s]
    m_ref[SHIFTS:16, :] = jnp.zeros((16 - SHIFTS, ROW_IMAGES), jnp.float32)
    peak = peaks[0]
    for s in range(1, SHIFTS):
        peak = jnp.maximum(peak, peaks[s])
    total = jnp.zeros((1, ROW_IMAGES), jnp.float32)
    for s in range(SHIFTS):
        total = total + sums[s] * jnp.exp(peaks[s] - peak)
    stats = jnp.concatenate(
        [
            peak[:, :LANES],
            peak[:, LANES:],
            total[:, :LANES],
            total[:, LANES:],
            jnp.zeros((4, LANES), jnp.float32),
        ],
        axis=0,
    )
    for k in range(8):
        st_ref[k] = stats


def far_kernel(shift_ref, e_ref, m_ref, all_ref, t_ref, out_ref, ev_ref, w_ref, tail_ref):
    x, core, _, _, _ = position()
    stats = [all_ref[k] for k in range(8)]
    peak = stats[0][0:2]
    for k in range(1, 8):
        peak = jnp.maximum(peak, stats[k][0:2])
    total = jnp.zeros((2, LANES), jnp.float32)
    for k in range(8):
        total = total + stats[k][2:4] * jnp.exp(stats[k][0:2] - peak)
    evidence = peak + jnp.log(total)
    slot = x * 2 + core
    mine = jnp.where(slot >= 4, evidence[1:2], evidence[0:1])
    groups = [mine[:, k * OWN : (k + 1) * OWN] for k in range(4)]
    at = jnp.bitwise_and(slot, 3)
    picked = groups[0]
    for k in range(1, 4):
        picked = jnp.where(at == k, groups[k], picked)
    ev_ref[...] = picked
    peak = jnp.concatenate([peak[0:1], peak[1:2]], axis=1)
    total = jnp.concatenate([total[0:1], total[1:2]], axis=1)

    for s in range(SHIFTS):
        factor = jnp.exp(m_ref[s : s + 1, :] - peak) / total
        weight = (e_ref[s] * factor).astype(jnp.bfloat16)
        w_ref[s * ROW_IMAGES : (s + 1) * ROW_IMAGES, :] = weight.T

    far = jnp.bitwise_and(position()[4] + 2, 3)
    acc = tile_sums(shift_ref, t_ref, w_ref, 0, far, ones=16)
    size = 2 * LANES * GROUP
    totals = acc[size : size + 1]
    totals = jnp.concatenate([totals, jnp.zeros((1, 2 * LANES - ROWS), jnp.float32)], axis=1)
    tail = split_tail(jnp.concatenate([totals[:, :LANES], totals[:, LANES:]], axis=0))
    tail_ref[...] = tail
    store_sums(out_ref, 0, acc[:size], tail)


GROUP = 4


def tile_sums(shift_ref, t_ref, w_ref, z, *ys, ones=0):
    tiles = []
    for y, k in [(y, k) for y in ys for k in range(GROUP)]:
        low = 2 * (4 * (z + k) + y)
        rows = (low, low + 1, low + 2 * 16, low + 2 * 16 + 1)
        tiles.append(
            jnp.concatenate(
                [
                    shifted_pixels(t_ref, rows, shift_ref[0, s], shift_ref[1, s])
                    for s in range(SHIFTS)
                ],
                axis=1,
            )
        )
    if ones:
        tiles.append(jnp.ones((ones, SHIFTS * ROW_IMAGES), jnp.bfloat16))
    moved = jnp.concatenate(tiles, axis=0)
    return jnp.dot(moved, w_ref[...], preferred_element_type=jnp.float32)


def is_tail():
    row = lax.broadcasted_iota(jnp.int32, (16, LANES), 0)
    return row >= USED - (ROWS - 16)


def store_sums(out_ref, z, acc, tail):
    turned = acc.astype(jnp.bfloat16).T
    for k in range(2 * GROUP):
        part = turned[:, k * LANES : (k + 1) * LANES]
        at = 4 * (k % 2) + z + k // 2
        out_ref[at, 0 : ROWS - 16, :] = part[: ROWS - 16]
        out_ref[at, ROWS - 16 : ROWS, :] = jnp.where(is_tail(), tail, part[ROWS - 16 :])


def near_kernel(shift_ref, w_ref, tail_ref, t_ref, up_ref, down_ref):
    y = position()[4]
    ahead, behind = jnp.bitwise_and(y + 1, 3), jnp.bitwise_and(y - 1, 3)
    size = 2 * LANES * GROUP
    for z in range(0, 4, GROUP):
        acc = tile_sums(shift_ref, t_ref, w_ref, z, ahead, behind)
        store_sums(up_ref, z, acc[:size], tail_ref[...])
        store_sums(down_ref, z, acc[size:], tail_ref[...])


def own_kernel(shift_ref, w_ref, t_ref, after_ref, out_ref):
    del after_ref
    y = position()[4]
    for z in range(0, 4, GROUP):
        turned = tile_sums(shift_ref, t_ref, w_ref, z, y).T
        for k in range(2 * GROUP):
            out_ref[4 * (k % 2) + z + k // 2] = turned[:, k * LANES : (k + 1) * LANES]


def split_tail(totals):
    pieces = []
    for _ in range(3):
        part = totals.astype(jnp.bfloat16).astype(jnp.float32)
        totals = totals - part
        pieces.append(part)
    lead = jnp.zeros((USED - (ROWS - 16), LANES), jnp.float32)
    rest = jnp.zeros((ROWS - USED - 6, LANES), jnp.float32)
    return jnp.concatenate([lead] + pieces + [rest], axis=0).astype(jnp.bfloat16)


def joined_tail(tail):
    at = USED - (ROWS - 16)
    return tail[at : at + 2] + tail[at + 2 : at + 4] + tail[at + 4 : at + 6]


def add_kernel(own_ref, tail_ref, far_ref, up_ref, down_ref, out_ref):
    others = (far_ref, up_ref, down_ref)
    totals = joined_tail(tail_ref[...].astype(jnp.float32))
    for ref in others:
        totals = totals + joined_tail(ref[0, ROWS - 16 : ROWS, :].astype(jnp.float32))
    tail = split_tail(totals)
    for k in range(8):
        acc = own_ref[k]
        for ref in others:
            acc = acc + ref[k].astype(jnp.float32)
        acc = acc.astype(jnp.bfloat16)
        out_ref[k, 0 : ROWS - 16, :] = acc[: ROWS - 16]
        out_ref[k, ROWS - 16 : ROWS, :] = jnp.where(is_tail(), tail, acc[ROWS - 16 :])


def finish_kernel(in_ref, out_ref, wt_ref):
    for half in range(2):
        acc = jnp.zeros((ROWS, LANES), jnp.float32)
        for k in range(4):
            acc = acc + in_ref[half * 4 + k].astype(jnp.float32)
        for r in range(HALF_ROT):
            out_ref[half * HALF_ROT + r] = acc[r * CLS : (r + 1) * CLS]
        wide = joined_tail(acc[ROWS - 16 :])
        totals = jnp.concatenate([wide[0:1], wide[1:2]], axis=1)
        for r in range(HALF_ROT):
            row = half * HALF_ROT + r
            wt_ref[row : row + 1, :] = totals[:, r * CLS : (r + 1) * CLS]


VMEM = pl.BlockSpec(memory_space=pltpu.VMEM)
SMEM = pl.BlockSpec(memory_space=pltpu.SMEM)
PARAMS = pltpu.CompilerParams(vmem_limit_bytes=40 * 1024 * 1024)


def cost(quarters, megabytes):
    flops = 1000 * quarters
    return pl.CostEstimate(flops=flops, bytes_accessed=1000 * megabytes, transcendentals=0)


def shards(particles, rot_prior, panels, log_prior, shift_table):
    spread, images, info = pl.pallas_call(
        prepare_kernel,
        out_shape=(
            jax.ShapeDtypeStruct((8, ROWS, LANES), jnp.bfloat16),
            jax.ShapeDtypeStruct((OWN, PIX + LANES), jnp.bfloat16),
            jax.ShapeDtypeStruct((ROWS, LANES), jnp.float32),
        ),
        in_specs=[pl.BlockSpec(memory_space=pltpu.HBM)] * 4,
        out_specs=(pl.BlockSpec(memory_space=pltpu.HBM),) * 3,
        scratch_shapes=[
            pltpu.VMEM((ROT, CLS, LANES), jnp.bfloat16),
            pltpu.VMEM((OWN, PIX), jnp.float32),
            pltpu.VMEM((1, OWN), jnp.int32),
            pltpu.VMEM((1, CLS), jnp.float32),
            pltpu.VMEM((2, ROWS, LANES), jnp.float32),
            pltpu.VMEM((8, ROWS, LANES), jnp.bfloat16),
            pltpu.VMEM((OWN, PIX + LANES), jnp.bfloat16),
            pltpu.VMEM((ROWS, LANES), jnp.float32),
            pltpu.SemaphoreType.DMA((4,)),
            pltpu.SemaphoreType.DMA((3,)),
        ],
        compiler_params=pltpu.CompilerParams(vmem_limit_bytes=60 * 1024 * 1024),
        cost_estimate=cost(0, 1),
        name="prepare",
    )(
        jnp.transpose(panels, (1, 0, 2)),
        particles,
        rot_prior.reshape(1, OWN),
        log_prior.reshape(1, CLS),
    )
    c0 = move(images, core=1)
    a1 = move(images, x=1)
    a2 = move(images, x=-1)
    a3 = move(images, x=2)
    column = lax.all_to_all(spread, "img", 0, 0, axis_index_groups=XZ_GROUPS)
    column, c0 = lax.optimization_barrier((column, c0))
    y1 = move(column, y=1)
    y3 = move(column, y=-1)
    mine = jnp.concatenate([a1, a2, a3], axis=0)
    mine, y1, y3 = lax.optimization_barrier((mine, y1, y3))
    cc = move(mine, core=1)
    yw0 = move(y1[:4], y=1)
    yw1 = move(y3[4:], y=-1)

    turned, rots = pl.pallas_call(
        turn_kernel,
        out_shape=(
            jax.ShapeDtypeStruct((2, SIDE, SIDE + 2 * MARGIN, LANES), jnp.float32),
            jax.ShapeDtypeStruct((2, 8, LANES), jnp.float32),
        ),
        in_specs=[VMEM] * 4,
        out_specs=(VMEM, VMEM),
        scratch_shapes=[pltpu.VMEM((ROW_IMAGES, PIX + LANES), jnp.bfloat16)],
        compiler_params=PARAMS,
        cost_estimate=cost(0, 8),
        name="turn",
    )(images, c0, mine, cc)

    shifts = shift_table.T
    score_shape = jax.ShapeDtypeStruct((SHIFTS, ROWS, ROW_IMAGES), jnp.float32)
    norm_shape = jax.ShapeDtypeStruct((ROWS, LANES), jnp.float32)
    scores, norms = pl.pallas_call(
        first_kernel,
        out_shape=(score_shape, norm_shape),
        in_specs=[SMEM] + [VMEM] * 4,
        out_specs=(VMEM, VMEM),
        compiler_params=PARAMS,
        cost_estimate=cost(3, 4),
        name="first",
    )(shifts, turned, column, y1, y3)

    scores, stats, peaks = pl.pallas_call(
        last_kernel,
        out_shape=(
            score_shape,
            jax.ShapeDtypeStruct((8, 8, LANES), jnp.float32),
            jax.ShapeDtypeStruct((16, ROW_IMAGES), jnp.float32),
        ),
        in_specs=[SMEM] + [VMEM] * 7,
        out_specs=(VMEM,) * 3,
        input_output_aliases={4: 0},
        compiler_params=PARAMS,
        cost_estimate=cost(1, 8),
        name="last",
    )(shifts, turned, yw0, yw1, scores, norms, rots, info)
    all_stats = lax.all_to_all(stats, AXES, 0, 0, axis_index_groups=X_ROWS)
    block_shape = jax.ShapeDtypeStruct((8, ROWS, LANES), jnp.bfloat16)
    far, evidence, weights, tail = pl.pallas_call(
        far_kernel,
        out_shape=(
            block_shape,
            jax.ShapeDtypeStruct((1, OWN), jnp.float32),
            jax.ShapeDtypeStruct((SHIFTS * ROW_IMAGES, ROWS), jnp.bfloat16),
            jax.ShapeDtypeStruct((16, LANES), jnp.bfloat16),
        ),
        in_specs=[SMEM] + [VMEM] * 4,
        out_specs=(VMEM,) * 4,
        compiler_params=PARAMS,
        cost_estimate=cost(1, 4),
        name="far",
    )(shifts, scores, peaks, all_stats, turned)
    from_far = move(far, y=2)
    up, down = pl.pallas_call(
        near_kernel,
        out_shape=(block_shape,) * 2,
        in_specs=[SMEM] + [VMEM] * 3,
        out_specs=(VMEM,) * 2,
        compiler_params=PARAMS,
        cost_estimate=cost(2, 4),
        name="near",
    )(shifts, weights, tail, turned)
    from_down = move(up, y=1)
    from_up = move(down, y=-1)
    own = pl.pallas_call(
        own_kernel,
        out_shape=jax.ShapeDtypeStruct((8, ROWS, LANES), jnp.float32),
        in_specs=[SMEM] + [VMEM] * 2 + [pl.BlockSpec(memory_space=pl.ANY)],
        out_specs=VMEM,
        compiler_params=PARAMS,
        cost_estimate=cost(1, 4),
        name="own",
    )(shifts, weights, turned, up)
    column_sums = pl.pallas_call(
        add_kernel,
        out_shape=block_shape,
        in_specs=[VMEM] * 5,
        out_specs=VMEM,
        compiler_params=PARAMS,
        cost_estimate=cost(0, 2),
        name="add",
    )(own, tail, from_far, from_down, from_up)
    shares = lax.all_to_all(column_sums, "img", 0, 0, axis_index_groups=XZ_GROUPS)
    sums, totals = pl.pallas_call(
        finish_kernel,
        out_shape=(
            jax.ShapeDtypeStruct((ROT, CLS, LANES), jnp.float32),
            jax.ShapeDtypeStruct((ROT, CLS), jnp.float32),
        ),
        in_specs=[VMEM],
        out_specs=(VMEM, VMEM),
        compiler_params=PARAMS,
        name="finish",
    )(shares)
    return jnp.transpose(sums, (1, 0, 2)), totals.T, evidence.reshape(OWN)


def solution(mesh):
    placed = (P(AXES, None), P(AXES), P("cls", None, "img"), P("cls"), P())
    return jax.shard_map(
        shards,
        mesh=mesh,
        in_specs=placed,
        out_specs=(P("cls", None, "img"), P("cls", None), P(AXES)),
        check_vma=False,
    )
```
